32 devices in a mesh: ctx: 8 (over z, x), head: 4 (over y, core).
Axes of the slice: x: 2, y: 2, z: 4, core: 2. Of those that a mesh axis runs over, the one named last changes fastest.
Arguments:
- queries: bfloat16 [1024, 4096], P('ctx', 'head'), may hold values from -6 to 6
- keys_new: bfloat16 [1024, 1024], P('ctx', 'head'), may hold values from -6 to 6
- values_new: bfloat16 [1024, 1024], P('ctx', 'head'), may hold values from -6 to 6
- cache_keys: bfloat16 [8192, 1024], P('ctx', 'head'), may hold values from -6 to 6
- cache_values: bfloat16 [8192, 1024], P('ctx', 'head'), may hold values from -6 to 6
- block_list: int32 [8, 8, 16], P('head', 'ctx'), may hold values from -1 to 63, as said below
- block_count: int32 [8, 8], P('head', 'ctx'), may hold values from 0 to 16
- out_weight: bfloat16 [4096, 4096], P('head'), may hold values from -0.21875 to 0.21875
Outputs:
- mixed: bfloat16 [1024, 4096], P(('ctx', 'head'))
The draws below stay inside these ranges and needn't reach their ends.
Inputs may be any that keep to these rules, and one draw needn't show every extreme that they name: `block_list`: row (h, q) holds distinct cache block numbers in increasing order in its first block_count[h, q] entries and -1 after them. For each KV head, the query blocks of one aligned run of 1 query block together list at most 2 blocks of each aligned run of 8 cache blocks and at least one; for every KV head some run lists exactly 2 of every run of cache blocks.
All inputs are finite; a program needn't handle non-finite values.
Results may differ from the reference program's by a relative error of at most 0.015.
Values may be sent and summed in bfloat16 or wider, within the bound.
A program may use at most 192 MiB of HBM per device.

```python
import jax
import jax.numpy as jnp
from jax import lax

D = 4096
HEADS = 32
KVH = 8
HD = 128
BLOCK = 128
CAP = 2
CB_DEV = 8
ROWS_DEV = 128
TOKENS = 1024
CACHE = 8192
QBLOCKS = 8
NBLOCKS = 64
SEL = 16


def block_choice(key):
    base_key = jax.random.fold_in(key, 11)
    split_keys = jax.random.split(base_key, 5)
    owners = NBLOCKS // CB_DEV
    qb_dev = ROWS_DEV // BLOCK
    taken_count = jax.random.randint(split_keys[0], (KVH, owners, owners), 1, CAP + 1)
    full_device = jax.random.randint(split_keys[1], (KVH,), 0, owners)
    is_full = jnp.arange(owners)[None, :] == full_device[:, None]
    taken_count = jnp.where(is_full[:, :, None], CAP, taken_count)
    scores = jax.random.randint(split_keys[2], (KVH, owners, owners, CB_DEV), 0, 1 << 20) * CB_DEV + jnp.arange(CB_DEV)
    block_rank = jnp.argsort(jnp.argsort(scores, axis=-1), axis=-1)
    union_mask = (block_rank < taken_count[..., None]).reshape(KVH, owners, NBLOCKS)
    levels = jax.random.randint(split_keys[3], (KVH, owners, qb_dev), 1, 9)
    first_block = (jnp.arange(qb_dev) == 0)[None, None, :]
    levels = jnp.where(is_full[:, :, None] & first_block, 8, levels)
    coin_flip = jax.random.randint(split_keys[4], (KVH, owners, qb_dev, NBLOCKS), 0, 8) < levels[..., None]
    block_ids = jnp.arange(NBLOCKS)
    covered = block_ids[None, :] % qb_dev == jnp.arange(qb_dev)[:, None]
    listed = (union_mask[:, :, None, :] & (coin_flip | covered[None, None])).reshape(KVH, QBLOCKS, NBLOCKS)
    counts = jnp.sum(listed.astype(jnp.int32), axis=-1).astype(jnp.int32)
    ordering = jnp.argsort(jnp.where(listed, block_ids, NBLOCKS + block_ids), axis=-1)
    leading = ordering[..., :SEL].astype(jnp.int32)
    slot_ids = jnp.arange(SEL)
    block_rows = jnp.where(slot_ids[None, None, :] < counts[..., None], leading, -1).astype(jnp.int32)
    return (block_rows, counts)


def draw_block_list(key, part):
    return block_choice(key)[0]


def draw_block_count(key, part):
    return block_choice(key)[1]


def draw_queries(key, part):
    result = jnp.clip(2.0 * jax.random.normal(jax.random.fold_in(key, 1), (TOKENS, HEADS * HD)), -6.0, 6.0)
    return result.astype(jnp.bfloat16)


def draw_keys_new(key, part):
    result = jnp.clip(jax.random.normal(jax.random.fold_in(key, 2), (TOKENS, KVH * HD)), -6.0, 6.0)
    return result.astype(jnp.bfloat16)


def block_levels(own_key, shape, pieces, smallest, largest):
    level = 1.0
    for dim, parts in pieces:
        heights = jax.random.uniform(jax.random.fold_in(jax.random.fold_in(own_key, 6), dim), (parts,), jnp.float32, smallest / len(pieces), largest / len(pieces))
        level = level * jnp.repeat(jnp.exp(heights), shape[dim] // parts).reshape((-1,) + (1,) * (len(shape) - 1 - dim))
    return level


def normal_values(own_key, shape, deviation, limit, shards=(), held_as=jnp.bfloat16):
    factor_of = block_levels(own_key, shape, shards, -0.22, 0.18) if shards else 1.0
    array = jax.random.normal(own_key, shape, jnp.float32) * deviation * factor_of
    return jnp.minimum(jnp.maximum(array, -limit), limit).astype(held_as)


def setup_inputs(seed: int = 0) -> dict:
    seeds = jax.random.split(jax.random.key(seed), 9)
    return {
        "queries": draw_queries(jax.random.fold_in(seeds[8], 71), 0),
        "keys_new": draw_keys_new(jax.random.fold_in(seeds[8], 71), 0),
        "values_new": normal_values(seeds[2], (TOKENS, KVH * HD), 1.0, 6.0, ((0, 8), (1, 4))),
        "cache_keys": normal_values(seeds[3], (CACHE, KVH * HD), 1.0, 6.0, ((0, 8), (1, 4))),
        "cache_values": normal_values(seeds[4], (CACHE, KVH * HD), 1.0, 6.0, ((0, 8), (1, 4))),
        "block_list": draw_block_list(jax.random.fold_in(seeds[8], 71), 0),
        "block_count": draw_block_count(jax.random.fold_in(seeds[8], 71), 0),
        "out_weight": normal_values(seeds[7], (HEADS * HD, D), (HEADS * HD // 6) ** -0.5, 0.21875, ((0, 4),)),
    }


def reference(queries, keys_new, values_new, cache_keys, cache_values, block_list, block_count, out_weight):
    nblocks = CACHE // BLOCK
    qblocks = TOKENS // BLOCK
    group_size = HEADS // KVH
    list_width = block_list.shape[2]
    cache_heads = cache_keys.reshape(nblocks, BLOCK, KVH, HD).transpose(2, 0, 1, 3)
    value_heads = cache_values.reshape(nblocks, BLOCK, KVH, HD).transpose(2, 0, 1, 3)
    stretch_keys = keys_new.reshape(qblocks, BLOCK, KVH, HD).transpose(2, 0, 1, 3)
    stretch_values = values_new.reshape(qblocks, BLOCK, KVH, HD).transpose(2, 0, 1, 3)
    query_blocks = queries.reshape(qblocks, BLOCK, KVH, group_size, HD)
    causal = jnp.arange(BLOCK)[:, None] >= jnp.arange(BLOCK)[None, :]
    score_scale = HD ** -0.5

    def one_block(block_index):
        block_rows = lax.dynamic_index_in_dim(block_list, block_index, 1, keepdims=False)
        counts = lax.dynamic_index_in_dim(block_count, block_index, 1, keepdims=False)
        in_use = jnp.arange(list_width)[None, :] < counts[:, None]
        safe_ids = jnp.where(in_use, block_rows, 0).astype(jnp.int32)
        key_rows = jax.vmap(lambda table, chosen: table[chosen])(cache_heads, safe_ids).reshape(KVH, list_width * BLOCK, HD)
        value_rows = jax.vmap(lambda table, chosen: table[chosen])(value_heads, safe_ids).reshape(KVH, list_width * BLOCK, HD)
        prev_block = jnp.maximum(block_index - 1, 0).astype(jnp.int32)
        prev_keys = lax.dynamic_index_in_dim(stretch_keys, prev_block, 1, keepdims=False)
        prev_values = lax.dynamic_index_in_dim(stretch_values, prev_block, 1, keepdims=False)
        own_keys = lax.dynamic_index_in_dim(stretch_keys, block_index, 1, keepdims=False)
        own_values = lax.dynamic_index_in_dim(stretch_values, block_index, 1, keepdims=False)
        all_keys = jnp.concatenate([key_rows, prev_keys, own_keys], axis=1).astype(jnp.float32)
        all_values = jnp.concatenate([value_rows, prev_values, own_values], axis=1).astype(jnp.float32)
        cache_ok = jnp.broadcast_to(jnp.repeat(in_use, BLOCK, axis=1)[:, None, :], (KVH, BLOCK, list_width * BLOCK))
        prev_ok = jnp.broadcast_to(block_index > 0, (KVH, BLOCK, BLOCK))
        own_ok = jnp.broadcast_to(causal, (KVH, BLOCK, BLOCK))
        allowed = jnp.concatenate([cache_ok, prev_ok, own_ok], axis=2)
        query_rows = lax.dynamic_index_in_dim(query_blocks, block_index, 0, keepdims=False).transpose(1, 2, 0, 3).astype(jnp.float32)
        scores = jnp.einsum('hgrd,hkd->hgrk', query_rows, all_keys) * score_scale
        scores = jnp.where(allowed[:, None], scores, -jnp.inf)
        row_max = jnp.max(scores, axis=-1, keepdims=True)
        weights = jnp.exp(scores - row_max)
        weight_sum = jnp.sum(weights, axis=-1, keepdims=True)
        rounded = lax.optimization_barrier(weights.astype(jnp.bfloat16)).astype(jnp.float32)
        mixture = jnp.einsum('hgrk,hkd->hgrd', rounded, all_values) / weight_sum
        return mixture.astype(jnp.bfloat16).transpose(2, 0, 1, 3).reshape(BLOCK, KVH * group_size * HD)

    attention = lax.map(one_block, jnp.arange(qblocks, dtype=jnp.int32)).reshape(TOKENS, HEADS * HD)
    return jnp.dot(attention, out_weight, preferred_element_type=jnp.float32).astype(jnp.bfloat16)
```

```python
import functools

import jax
import jax.numpy as jnp
from jax import lax
from jax.experimental import pallas as pl
from jax.experimental.pallas import tpu as pltpu
from jax.sharding import PartitionSpec as P

HD = 128
BLOCK = 128
CAP = 2
CB_DEV = 8
GROUPS = 2
PARTS = 4
NEG = -1e30
EXP2_SCALE = HD**-0.5 * 1.4426950408889634
F32 = jnp.float32
BF16 = jnp.bfloat16


def remote(src, dst, send_sem, recv_sem, device):
    return pltpu.make_async_remote_copy(
        src_ref=src,
        dst_ref=dst,
        send_sem=send_sem,
        recv_sem=recv_sem,
        device_id=device,
        device_id_type=pl.DeviceIdType.MESH,
    )


def kernel(
    n, n_head, kvh, group,
    list_ref, count_ref, q_ref, kn_ref, vn_ref, ck_ref, cv_ref, w_hbm,
    out_ref,
    table, meta, meta_s, far_table, far_q, prev, qstack, sendb, recvb, acc, stat,
    part_out, part_in, stat_in, att, w_v, proj, proj16, r1, s2, r2,
    meta_ss, meta_rs, smem_s, kv_ss, kv_rs, prev_ss, prev_rs, far_ss, far_rs,
    back_ss, back_rs, w_sem, p1_ss, p1_rs, p2_ss, p2_rs,
):
    me = lax.axis_index("ctx")
    hi = lax.axis_index("head")
    half = n // GROUPS
    mypos = lax.rem(me, half)
    base = me - mypos
    mirror = lax.rem(me + half, n)
    cols = w_v.shape[2]

    def w_copy(c):
        return pltpu.make_async_copy(
            w_hbm.at[:, pl.ds(c * cols, cols)], w_v.at[c], w_sem.at[c]
        )

    barrier = pltpu.get_barrier_semaphore()
    for k in range(1, n):
        pl.semaphore_signal(
            barrier, inc=1, device_id={"ctx": lax.rem(me + k, n)},
            device_id_type=pl.DeviceIdType.MESH,
        )
    for k in range(1, n_head):
        pl.semaphore_signal(
            barrier, inc=1, device_id={"head": lax.rem(hi + k, n_head)},
            device_id_type=pl.DeviceIdType.MESH,
        )

    blk = list_ref[...]
    lane = lax.broadcasted_iota(jnp.int32, blk.shape, 1)
    used = jnp.where(lane < count_ref[...], blk, -1)
    for o in range(n):
        mine = (used >= o * CB_DEV) & (used < (o + 1) * CB_DEV)
        first = jnp.min(jnp.where(mine, used - o * CB_DEV, CB_DEV - 1), axis=1, keepdims=True)
        last = jnp.max(jnp.where(mine, used - o * CB_DEV, 0), axis=1, keepdims=True)
        two = (last > first).astype(jnp.int32)
        table[o, 0:kvh, :] = jnp.broadcast_to(first, (kvh, 128))
        table[o, kvh : 2 * kvh, :] = jnp.broadcast_to(last, (kvh, 128))
        table[o, 2 * kvh : 3 * kvh, :] = jnp.broadcast_to(two, (kvh, 128))

    pl.semaphore_wait(barrier, n - 1 + n_head - 1)

    def meta_send(k):
        d = lax.rem(me + k, n)
        return remote(table.at[d], meta.at[me], meta_ss.at[k], meta_rs.at[me], {"ctx": d})

    def meta_recv(d):
        return remote(table.at[d], meta.at[d], meta_ss.at[0], meta_rs.at[d], {"ctx": mirror})

    for k in range(1, n):
        meta_send(k).start()
    far_copies = []
    if GROUPS == 2:
        far_copies = [
            remote(table, far_table, far_ss.at[0], far_rs.at[0], {"ctx": mirror}),
            remote(q_ref, far_q, far_ss.at[1], far_rs.at[1], {"ctx": mirror}),
        ]
    for copy in far_copies:
        copy.start()
    nxt = lax.rem(me + 1, n)
    prev_copies = [
        remote(kn_ref, prev.at[0], prev_ss.at[0], prev_rs.at[0], {"ctx": nxt}),
        remote(vn_ref, prev.at[1], prev_ss.at[1], prev_rs.at[1], {"ctx": nxt}),
    ]

    def own_smem():
        return pltpu.make_async_copy(table.at[me], meta_s.at[me], smem_s.at[me])

    own_smem().start()

    def smem_copy(d):
        return pltpu.make_async_copy(meta.at[d], meta_s.at[d], smem_s.at[d])

    def target(x, k):
        pi = lax.rem(mypos + k, half)
        p = base + pi
        d = p if x == 0 else lax.rem(p + half, n)
        return pi, p, d

    def gather(d, dst):
        for h in range(kvh):
            for s in range(CAP):
                index = meta_s[d, s * kvh + h, 0]
                cut = slice(h * HD, (h + 1) * HD)
                dst[h, 0, s * BLOCK : (s + 1) * BLOCK, :] = ck_ref[index, :, cut]
                dst[h, 1, s * BLOCK : (s + 1) * BLOCK, :] = cv_ref[index, :, cut]

    def kv_send(x, k):
        pi, p, _ = target(x, k)
        return remote(
            sendb.at[x, pi], recvb.at[x, mypos], kv_ss.at[x, pi], kv_rs.at[x, mypos], {"ctx": p}
        )

    def kv_recv(x, k):
        pi, p, _ = target(x, half - k)
        return pi, remote(
            sendb.at[x, pi], recvb.at[x, pi], kv_ss.at[x, pi], kv_rs.at[x, pi], {"ctx": p}
        )

    order = list(range(GROUPS))[::-1]
    for x in order:
        def fetch(k, _, x=x):
            _, _, d = target(x, k)
            meta_recv(d).wait_recv()
            smem_copy(d).start()
            return 0

        lax.fori_loop(1, half, fetch, 0)
    if GROUPS == 2:
        meta_recv(mirror).wait_recv()
        smem_copy(mirror).start()
    for x in order:
        def give(k, _, x=x):
            pi, _, d = target(x, k)
            smem_copy(d).wait()
            gather(d, sendb.at[x, pi])
            kv_send(x, k).start()
            return 0

        lax.fori_loop(1, half, give, 0)
        if x == order[0]:
            for copy in prev_copies:
                @pl.when(me < n - 1)
                def _(copy=copy):
                    copy.start()

    for copy_c in range(PARTS):
        w_copy(copy_c).start()
    own_smem().wait()
    gather(me, recvb.at[0, mypos])
    if GROUPS == 2:
        smem_copy(mirror).wait()
        gather(mirror, recvb.at[1, mypos])

    width = group * BLOCK

    def stack(x, ref):
        for h in range(kvh):
            for j in range(group):
                column = (h * group + j) * HD
                qstack[x, h, j * BLOCK : (j + 1) * BLOCK, :] = ref[:, column : column + HD]

    def attend(x, h, keys, values, mask):
        scores = lax.dot_general(
            keys, qstack[x, h], (((1,), (1,)), ((), ())), preferred_element_type=F32
        )
        scores = mask(scores)
        old_max = stat[x, h : h + 1, :]
        new_max = jnp.maximum(old_max, jnp.max(scores, axis=0, keepdims=True))
        weights = jnp.exp2((scores - new_max) * EXP2_SCALE)
        fade = jnp.exp2((old_max - new_max) * EXP2_SCALE)
        total = stat[x, kvh + h : kvh + h + 1, :] * fade
        stat[x, h : h + 1, :] = new_max
        stat[x, kvh + h : kvh + h + 1, :] = total + jnp.sum(weights, axis=0, keepdims=True)
        mixture = lax.dot_general(
            values, weights.astype(BF16), (((0,), (0,)), ((), ())), preferred_element_type=F32
        )
        acc[x, h] = acc[x, h] * fade + mixture

    def attend_cache(x, pi):
        flags = table if x == 0 else far_table
        for h in range(kvh):
            two = flags[base + pi, 2 * kvh + h : 2 * kvh + h + 1, :]
            two = jnp.concatenate([two] * group, axis=1)

            def mask(scores):
                return jnp.concatenate(
                    [scores[:BLOCK], jnp.where(two > 0, scores[BLOCK:], NEG)], axis=0
                )

            attend(x, h, recvb[x, pi, h, 0], recvb[x, pi, h, 1], mask)

    def attend_arrivals(x):
        def step(k, _):
            pi, copy = kv_recv(x, k)
            copy.wait_recv()
            attend_cache(x, pi)
            return 0

        lax.fori_loop(1, half, step, 0)

    stat[:, 0:kvh, :] = jnp.full((GROUPS, kvh, width), NEG, F32)
    stat[:, kvh:, :] = jnp.zeros((GROUPS, stat.shape[1] - kvh, width), F32)
    acc[...] = jnp.zeros_like(acc)
    stack(0, q_ref)

    def causal(scores):
        key = lax.broadcasted_iota(jnp.int32, scores.shape, 0)
        row = lax.broadcasted_iota(jnp.int32, scores.shape, 1) & (BLOCK - 1)
        return jnp.where(key <= row, scores, NEG)

    for h in range(kvh):
        cut = slice(h * HD, (h + 1) * HD)
        attend(0, h, kn_ref[:, cut], vn_ref[:, cut], causal)
    attend_cache(0, mypos)

    back_copies = []
    if GROUPS == 2:
        for copy in far_copies:
            copy.wait_recv()
        stack(1, far_q)
        attend_cache(1, mypos)
        attend_arrivals(1)
        part_out[...] = acc[1].astype(BF16)
        back_copies = [
            remote(stat.at[1], stat_in, back_ss.at[0], back_rs.at[0], {"ctx": mirror}),
            remote(part_out, part_in, back_ss.at[1], back_rs.at[1], {"ctx": mirror}),
        ]
        for copy in back_copies:
            copy.start()

    @pl.when(me > 0)
    def _():
        for copy in prev_copies:
            copy.wait_recv()
        for h in range(kvh):
            cut = slice(h * HD, (h + 1) * HD)
            attend(0, h, prev[0, :, cut], prev[1, :, cut], lambda scores: scores)

    attend_arrivals(0)
    for copy in back_copies:
        copy.wait_recv()
    for h in range(kvh):
        own = acc[0, h]
        total = stat[0, kvh + h : kvh + h + 1, :]
        if GROUPS == 2:
            here, there = stat[0, h : h + 1, :], stat_in[h : h + 1, :]
            top = jnp.maximum(here, there)
            fade_here = jnp.exp2((here - top) * EXP2_SCALE)
            fade_there = jnp.exp2((there - top) * EXP2_SCALE)
            own = own * fade_here + part_in[h].astype(F32) * fade_there
            total = total * fade_here + stat_in[kvh + h : kvh + h + 1, :] * fade_there
        own = own / total
        for j in range(group):
            column = (h * group + j) * HD
            block = own[:, j * BLOCK : (j + 1) * BLOCK]
            att[:, column : column + HD] = block.T.astype(BF16)

    core = lax.rem(hi, 2)
    row = hi // 2
    core_peer = hi + 1 - 2 * core
    row_peer = lax.rem(hi + 2, n_head)
    piece = BLOCK // n_head

    def to_core(c):
        return remote(
            proj16.at[c, 1 - core], r1.at[c], p1_ss.at[c], p1_rs.at[c], {"head": core_peer}
        )

    def to_row(c):
        return remote(s2.at[c], r2.at[c], p2_ss.at[c], p2_rs.at[c], {"head": row_peer})

    def forward(c):
        to_core(c).wait_recv()
        s2[c] = (proj[c, core, 1 - row] + r1[c, 1 - row].astype(F32)).astype(BF16)
        to_row(c).start()

    for c in range(PARTS):
        w_copy(c).wait()
        product = jnp.dot(att[...], w_v[c], preferred_element_type=F32)
        for i in range(n_head):
            rows = product[i * piece : (i + 1) * piece]
            proj[c, i % 2, i // 2] = rows
            proj16[c, i % 2, i // 2] = rows.astype(BF16)
        to_core(c).start()
        if c > 0:
            forward(c - 1)
    forward(PARTS - 1)
    for c in range(PARTS):
        to_row(c).wait_recv()
        out_ref[:, c * cols : (c + 1) * cols] = (
            proj[c, core, row] + r1[c, row].astype(F32) + r2[c].astype(F32)
        ).astype(BF16)

    for k in range(1, n):
        meta_send(k).wait_send()
    for copy in far_copies + back_copies:
        copy.wait_send()
    for copy in prev_copies:
        @pl.when(me < n - 1)
        def _(copy=copy):
            copy.wait_send()
    for x in range(GROUPS):
        def sent(k, _, x=x):
            kv_send(x, k).wait_send()
            return 0

        lax.fori_loop(1, half, sent, 0)
    for c in range(PARTS):
        to_core(c).wait_send()
        to_row(c).wait_send()


def shards(
    queries, keys_new, values_new, cache_keys, cache_values, block_list, block_count, out_weight
):
    n = lax.axis_size("ctx")
    n_head = lax.axis_size("head")
    kvh = keys_new.shape[1] // HD
    group = queries.shape[1] // keys_new.shape[1]
    half = n // GROUPS
    width = group * BLOCK
    d_in, d_out = out_weight.shape
    cols = d_out // PARTS
    piece = BLOCK // n_head
    vmem, any_space = pl.BlockSpec(memory_space=pltpu.VMEM), pl.BlockSpec(memory_space=pl.ANY)
    dma = pltpu.SemaphoreType.DMA
    keys_slot = CAP * BLOCK
    scratch = [
        pltpu.VMEM((n, 8, 128), jnp.int32),
        pltpu.VMEM((n, 8, 128), jnp.int32),
        pltpu.SMEM((n, 8, 128), jnp.int32),
        pltpu.VMEM((n, 8, 128), jnp.int32),
        pltpu.VMEM(queries.shape, BF16),
        pltpu.VMEM((2,) + keys_new.shape, BF16),
        pltpu.VMEM((GROUPS, kvh, width, HD), BF16),
        pltpu.VMEM((GROUPS, half, kvh, 2, keys_slot, HD), BF16),
        pltpu.VMEM((GROUPS, half, kvh, 2, keys_slot, HD), BF16),
        pltpu.VMEM((GROUPS, kvh, HD, width), F32),
        pltpu.VMEM((GROUPS, 8, width), F32),
        pltpu.VMEM((kvh, HD, width), BF16),
        pltpu.VMEM((kvh, HD, width), BF16),
        pltpu.VMEM((8, width), F32),
        pltpu.VMEM((BLOCK, d_in), BF16),
        pltpu.VMEM((PARTS, d_in, cols), BF16),
        pltpu.VMEM((PARTS, 2, n_head // 2, piece, cols), F32),
        pltpu.VMEM((PARTS, 2, n_head // 2, piece, cols), BF16),
        pltpu.VMEM((PARTS, n_head // 2, piece, cols), BF16),
        pltpu.VMEM((PARTS, piece, cols), BF16),
        pltpu.VMEM((PARTS, piece, cols), BF16),
        dma((n,)), dma((n,)), dma((n,)),
        dma((GROUPS, half)), dma((GROUPS, half)),
        dma((2,)), dma((2,)), dma((2,)), dma((2,)), dma((2,)), dma((2,)),
        dma((PARTS,)), dma((PARTS,)), dma((PARTS,)), dma((PARTS,)), dma((PARTS,)),
    ]
    return pl.pallas_call(
        functools.partial(kernel, n, n_head, kvh, group),
        out_shape=jax.ShapeDtypeStruct((piece, d_out), BF16),
        in_specs=[vmem] * 7 + [any_space],
        out_specs=vmem,
        scratch_shapes=scratch,
        compiler_params=pltpu.CompilerParams(
            collective_id=0, has_side_effects=True, vmem_limit_bytes=56 * 2**20
        ),
    )(
        block_list.reshape(kvh, -1), block_count.reshape(kvh, 1),
        queries, keys_new, values_new,
        cache_keys.reshape(CB_DEV, BLOCK, -1), cache_values.reshape(CB_DEV, BLOCK, -1), out_weight,
    )


def solution(mesh):
    return jax.shard_map(
        shards,
        mesh=mesh,
        in_specs=(
            P("ctx", "head"),
            P("ctx", "head"),
            P("ctx", "head"),
            P("ctx", "head"),
            P("ctx", "head"),
            P("head", "ctx", None),
            P("head", "ctx"),
            P("head", None),
        ),
        out_specs=P(("ctx", "head"), None),
        check_vma=False,
    )
```

```python
import functools

import jax
import jax.numpy as jnp
from jax import lax
from jax.experimental import pallas as pl
from jax.experimental.pallas import tpu as pltpu
from jax.sharding import PartitionSpec as P

HD = 128
BLOCK = 128
CAP = 2
CB_DEV = 8
GROUPS = 2
PARTS = 4
NEG = -1e30
EXP2_SCALE = HD**-0.5 * 1.4426950408889634
F32 = jnp.float32
BF16 = jnp.bfloat16


def remote(src, dst, send_sem, recv_sem, device):
    return pltpu.make_async_remote_copy(
        src_ref=src,
        dst_ref=dst,
        send_sem=send_sem,
        recv_sem=recv_sem,
        device_id=device,
        device_id_type=pl.DeviceIdType.MESH,
    )


def kernel(
    n, n_head, kvh, group,
    list_ref, count_ref, q_ref, kn_ref, vn_ref, ck_ref, cv_ref, w_hbm,
    out_ref,
    table, meta, meta_s, far_table, far_q, prev, qstack, sendb, recvb, acc, stat,
    part_out, part_in, stat_in, att, w_v, proj, proj16, r1, s2, r2,
    meta_ss, meta_rs, smem_s, kv_ss, kv_rs, prev_ss, prev_rs, far_ss, far_rs,
    back_ss, back_rs, w_sem, p1_ss, p1_rs, p2_ss, p2_rs,
):
    me = lax.axis_index("ctx")
    hi = lax.axis_index("head")
    half = n // GROUPS
    mypos = lax.rem(me, half)
    base = me - mypos
    mirror = lax.rem(me + half, n)
    cols = w_v.shape[2]

    def w_copy(c):
        return pltpu.make_async_copy(
            w_hbm.at[:, pl.ds(c * cols, cols)], w_v.at[c], w_sem.at[c]
        )

    barrier = pltpu.get_barrier_semaphore()
    for k in range(1, n):
        pl.semaphore_signal(
            barrier, inc=1, device_id={"ctx": lax.rem(me + k, n)},
            device_id_type=pl.DeviceIdType.MESH,
        )
    for k in range(1, n_head):
        pl.semaphore_signal(
            barrier, inc=1, device_id={"head": lax.rem(hi + k, n_head)},
            device_id_type=pl.DeviceIdType.MESH,
        )

    blk = list_ref[...]
    lane = lax.broadcasted_iota(jnp.int32, blk.shape, 1)
    head = lax.broadcasted_iota(jnp.int32, blk.shape, 0)
    used = jnp.full_like(blk, -1)
    for h in range(kvh):
        used = jnp.where((head == h) & (lane < count_ref[0, h]), blk, used)
    for o in range(n):
        mine = (used >= o * CB_DEV) & (used < (o + 1) * CB_DEV)
        first = jnp.min(jnp.where(mine, used - o * CB_DEV, CB_DEV - 1), axis=1, keepdims=True)
        last = jnp.max(jnp.where(mine, used - o * CB_DEV, 0), axis=1, keepdims=True)
        two = (last > first).astype(jnp.int32)
        table[o, 0:kvh, :] = jnp.broadcast_to(first, (kvh, 128))
        table[o, kvh : 2 * kvh, :] = jnp.broadcast_to(last, (kvh, 128))
        table[o, 2 * kvh : 3 * kvh, :] = jnp.broadcast_to(two, (kvh, 128))

    pl.semaphore_wait(barrier, n - 1 + n_head - 1)

    def meta_send(k):
        d = lax.rem(me + k, n)
        return remote(table.at[d], meta.at[me], meta_ss.at[k], meta_rs.at[me], {"ctx": d})

    def meta_recv(d):
        return remote(table.at[d], meta.at[d], meta_ss.at[0], meta_rs.at[d], {"ctx": mirror})

    for k in range(1, n):
        meta_send(k).start()
    far_copies = []
    if GROUPS == 2:
        far_copies = [
            remote(table, far_table, far_ss.at[0], far_rs.at[0], {"ctx": mirror}),
            remote(q_ref, far_q, far_ss.at[1], far_rs.at[1], {"ctx": mirror}),
        ]
    for copy in far_copies:
        copy.start()
    nxt = lax.rem(me + 1, n)
    prev_copies = [
        remote(kn_ref, prev.at[0], prev_ss.at[0], prev_rs.at[0], {"ctx": nxt}),
        remote(vn_ref, prev.at[1], prev_ss.at[1], prev_rs.at[1], {"ctx": nxt}),
    ]

    def own_smem():
        return pltpu.make_async_copy(table.at[me], meta_s.at[me], smem_s.at[me])

    own_smem().start()

    def smem_copy(d):
        return pltpu.make_async_copy(meta.at[d], meta_s.at[d], smem_s.at[d])

    def partner(k):
        place, total = 1, 0
        while place < half:
            a, b = lax.rem(mypos // place, 2), lax.rem(k // place, 2)
            total = total + place * (a + b - 2 * a * b)
            place *= 2
        return total

    def target(x, k):
        pi = partner(k)
        p = base + pi
        d = p if x == 0 else lax.rem(p + half, n)
        return pi, p, d

    def gather(d, dst):
        for h in range(kvh):
            for s in range(CAP):
                index = meta_s[d, s * kvh + h, 0]
                cut = slice(h * HD, (h + 1) * HD)
                dst[h, 0, s * BLOCK : (s + 1) * BLOCK, :] = ck_ref[index, :, cut]
                dst[h, 1, s * BLOCK : (s + 1) * BLOCK, :] = cv_ref[index, :, cut]

    def kv_send(x, k):
        pi, p, _ = target(x, k)
        return remote(
            sendb.at[x, pi], recvb.at[x, mypos], kv_ss.at[x, pi], kv_rs.at[x, mypos], {"ctx": p}
        )

    def kv_recv(x, k):
        pi, p, _ = target(x, k)
        return pi, remote(
            sendb.at[x, pi], recvb.at[x, pi], kv_ss.at[x, pi], kv_rs.at[x, pi], {"ctx": p}
        )

    order = list(range(GROUPS))[::-1]
    for x in order:
        def fetch(k, _, x=x):
            _, _, d = target(x, k)
            meta_recv(d).wait_recv()
            smem_copy(d).start()
            return 0

        lax.fori_loop(1, half, fetch, 0)
    if GROUPS == 2:
        meta_recv(mirror).wait_recv()
        smem_copy(mirror).start()
    for x in order:
        def give(k, _, x=x):
            pi, _, d = target(x, k)
            smem_copy(d).wait()
            gather(d, sendb.at[x, pi])
            if x == order[0]:
                kv_send(x, k).start()
            return 0

        lax.fori_loop(1, half, give, 0)

    for copy_c in range(PARTS):
        w_copy(copy_c).start()
    own_smem().wait()
    gather(me, recvb.at[0, mypos])
    if GROUPS == 2:
        smem_copy(mirror).wait()
        gather(mirror, recvb.at[1, mypos])

    width = group * BLOCK

    def stack(x, ref):
        for h in range(kvh):
            for j in range(group):
                column = (h * group + j) * HD
                qstack[x, h, j * BLOCK : (j + 1) * BLOCK, :] = ref[:, column : column + HD]

    def attend(x, h, keys, values, mask):
        scores = lax.dot_general(
            keys, qstack[x, h], (((1,), (1,)), ((), ())), preferred_element_type=F32
        )
        scores = mask(scores)
        old_max = stat[x, h : h + 1, :]
        new_max = jnp.maximum(old_max, jnp.max(scores, axis=0, keepdims=True))
        weights = jnp.exp2((scores - new_max) * EXP2_SCALE)
        fade = jnp.exp2((old_max - new_max) * EXP2_SCALE)
        total = stat[x, kvh + h : kvh + h + 1, :] * fade
        stat[x, h : h + 1, :] = new_max
        stat[x, kvh + h : kvh + h + 1, :] = total + jnp.sum(weights, axis=0, keepdims=True)
        mixture = lax.dot_general(
            values, weights.astype(BF16), (((0,), (0,)), ((), ())), preferred_element_type=F32
        )
        acc[x, h] = acc[x, h] * fade + mixture

    def attend_cache(x, pi):
        flags = table if x == 0 else far_table
        for h in range(kvh):
            two = flags[base + pi, 2 * kvh + h : 2 * kvh + h + 1, :]
            two = jnp.concatenate([two] * group, axis=1)

            def mask(scores):
                return jnp.concatenate(
                    [scores[:BLOCK], jnp.where(two > 0, scores[BLOCK:], NEG)], axis=0
                )

            attend(x, h, recvb[x, pi, h, 0], recvb[x, pi, h, 1], mask)

    def attend_arrivals(x):
        def step(k, _):
            pi, copy = kv_recv(x, k)
            copy.wait_recv()
            attend_cache(x, pi)
            if x != order[-1]:
                kv_send(x, k).wait_send()
                kv_send(x - 1, k).start()
            return 0

        lax.fori_loop(1, half, step, 0)

    stat[:, 0:kvh, :] = jnp.full((GROUPS, kvh, width), NEG, F32)
    stat[:, kvh:, :] = jnp.zeros((GROUPS, stat.shape[1] - kvh, width), F32)
    acc[...] = jnp.zeros_like(acc)
    stack(0, q_ref)

    def causal(scores):
        key = lax.broadcasted_iota(jnp.int32, scores.shape, 0)
        row = lax.broadcasted_iota(jnp.int32, scores.shape, 1) & (BLOCK - 1)
        return jnp.where(key <= row, scores, NEG)

    for h in range(kvh):
        cut = slice(h * HD, (h + 1) * HD)
        attend(0, h, kn_ref[:, cut], vn_ref[:, cut], causal)
    attend_cache(0, mypos)

    back_copies = []
    if GROUPS == 2:
        for copy in far_copies:
            copy.wait_recv()
        stack(1, far_q)
        attend_cache(1, mypos)
        attend_arrivals(1)
        part_out[...] = acc[1].astype(BF16)
        back_copies = [
            remote(stat.at[1], stat_in, back_ss.at[0], back_rs.at[0], {"ctx": mirror}),
            remote(part_out, part_in, back_ss.at[1], back_rs.at[1], {"ctx": mirror}),
        ]
        for copy in back_copies:
            copy.start()
    for copy in prev_copies:
        @pl.when(me < n - 1)
        def _(copy=copy):
            copy.start()

    @pl.when(me > 0)
    def _():
        for copy in prev_copies:
            copy.wait_recv()
        for h in range(kvh):
            cut = slice(h * HD, (h + 1) * HD)
            attend(0, h, prev[0, :, cut], prev[1, :, cut], lambda scores: scores)

    attend_arrivals(0)
    for copy in back_copies:
        copy.wait_recv()
    for h in range(kvh):
        own = acc[0, h]
        total = stat[0, kvh + h : kvh + h + 1, :]
        if GROUPS == 2:
            here, there = stat[0, h : h + 1, :], stat_in[h : h + 1, :]
            top = jnp.maximum(here, there)
            fade_here = jnp.exp2((here - top) * EXP2_SCALE)
            fade_there = jnp.exp2((there - top) * EXP2_SCALE)
            own = own * fade_here + part_in[h].astype(F32) * fade_there
            total = total * fade_here + stat_in[kvh + h : kvh + h + 1, :] * fade_there
        own = own / total
        for j in range(group):
            column = (h * group + j) * HD
            block = own[:, j * BLOCK : (j + 1) * BLOCK]
            att[:, column : column + HD] = block.T.astype(BF16)

    core = lax.rem(hi, 2)
    row = hi // 2
    core_peer = hi + 1 - 2 * core
    row_peer = lax.rem(hi + 2, n_head)
    piece = BLOCK // n_head

    def to_core(c):
        return remote(
            proj16.at[c, 1 - core], r1.at[c], p1_ss.at[c], p1_rs.at[c], {"head": core_peer}
        )

    def to_row(c):
        return remote(s2.at[c], r2.at[c], p2_ss.at[c], p2_rs.at[c], {"head": row_peer})

    def forward(c):
        to_core(c).wait_recv()
        s2[c] = (proj[c, core, 1 - row] + r1[c, 1 - row].astype(F32)).astype(BF16)
        to_row(c).start()

    for c in range(PARTS):
        w_copy(c).wait()
        product = jnp.dot(att[...], w_v[c], preferred_element_type=F32)
        for i in range(n_head):
            rows = product[i * piece : (i + 1) * piece]
            proj[c, i % 2, i // 2] = rows
            proj16[c, i % 2, i // 2] = rows.astype(BF16)
        to_core(c).start()
        if c > 0:
            forward(c - 1)
    forward(PARTS - 1)
    for c in range(PARTS):
        to_row(c).wait_recv()
        out_ref[:, c * cols : (c + 1) * cols] = (
            proj[c, core, row] + r1[c, row].astype(F32) + r2[c].astype(F32)
        ).astype(BF16)

    for k in range(1, n):
        meta_send(k).wait_send()
    for copy in far_copies + back_copies:
        copy.wait_send()
    for copy in prev_copies:
        @pl.when(me < n - 1)
        def _(copy=copy):
            copy.wait_send()
    def sent(k, _):
        kv_send(0, k).wait_send()
        return 0

    lax.fori_loop(1, half, sent, 0)
    for c in range(PARTS):
        to_core(c).wait_send()
        to_row(c).wait_send()


def shards(
    queries, keys_new, values_new, cache_keys, cache_values, block_list, block_count, out_weight
):
    n = lax.axis_size("ctx")
    n_head = lax.axis_size("head")
    kvh = keys_new.shape[1] // HD
    group = queries.shape[1] // keys_new.shape[1]
    half = n // GROUPS
    width = group * BLOCK
    d_in, d_out = out_weight.shape
    cols = d_out // PARTS
    piece = BLOCK // n_head
    vmem, any_space = pl.BlockSpec(memory_space=pltpu.VMEM), pl.BlockSpec(memory_space=pl.ANY)
    smem = pl.BlockSpec(memory_space=pltpu.SMEM)
    dma = pltpu.SemaphoreType.DMA
    keys_slot = CAP * BLOCK
    scratch = [
        pltpu.VMEM((n, 8, 128), jnp.int32),
        pltpu.VMEM((n, 8, 128), jnp.int32),
        pltpu.SMEM((n, 8, 128), jnp.int32),
        pltpu.VMEM((n, 8, 128), jnp.int32),
        pltpu.VMEM(queries.shape, BF16),
        pltpu.VMEM((2,) + keys_new.shape, BF16),
        pltpu.VMEM((GROUPS, kvh, width, HD), BF16),
        pltpu.VMEM((GROUPS, half, kvh, 2, keys_slot, HD), BF16),
        pltpu.VMEM((GROUPS, half, kvh, 2, keys_slot, HD), BF16),
        pltpu.VMEM((GROUPS, kvh, HD, width), F32),
        pltpu.VMEM((GROUPS, 8, width), F32),
        pltpu.VMEM((kvh, HD, width), BF16),
        pltpu.VMEM((kvh, HD, width), BF16),
        pltpu.VMEM((8, width), F32),
        pltpu.VMEM((BLOCK, d_in), BF16),
        pltpu.VMEM((PARTS, d_in, cols), BF16),
        pltpu.VMEM((PARTS, 2, n_head // 2, piece, cols), F32),
        pltpu.VMEM((PARTS, 2, n_head // 2, piece, cols), BF16),
        pltpu.VMEM((PARTS, n_head // 2, piece, cols), BF16),
        pltpu.VMEM((PARTS, piece, cols), BF16),
        pltpu.VMEM((PARTS, piece, cols), BF16),
        dma((n,)), dma((n,)), dma((n,)),
        dma((GROUPS, half)), dma((GROUPS, half)),
        dma((2,)), dma((2,)), dma((2,)), dma((2,)), dma((2,)), dma((2,)),
        dma((PARTS,)), dma((PARTS,)), dma((PARTS,)), dma((PARTS,)), dma((PARTS,)),
    ]
    return pl.pallas_call(
        functools.partial(kernel, n, n_head, kvh, group),
        out_shape=jax.ShapeDtypeStruct((piece, d_out), BF16),
        in_specs=[vmem, smem] + [vmem] * 5 + [any_space],
        out_specs=vmem,
        scratch_shapes=scratch,
        compiler_params=pltpu.CompilerParams(
            collective_id=0, has_side_effects=True, vmem_limit_bytes=56 * 2**20
        ),
    )(
        block_list.reshape(kvh, -1), block_count.reshape(1, kvh),
        queries, keys_new, values_new,
        cache_keys.reshape(CB_DEV, BLOCK, -1), cache_values.reshape(CB_DEV, BLOCK, -1), out_weight,
    )


def solution(mesh):
    return jax.shard_map(
        shards,
        mesh=mesh,
        in_specs=(
            P("ctx", "head"),
            P("ctx", "head"),
            P("ctx", "head"),
            P("ctx", "head"),
            P("ctx", "head"),
            P("head", "ctx", None),
            P("head", "ctx"),
            P("head", None),
        ),
        out_specs=P(("ctx", "head"), None),
        check_vma=False,
    )
```

```python
import functools

import jax
import jax.numpy as jnp
from jax import lax
from jax.experimental import pallas as pl
from jax.experimental.pallas import tpu as pltpu
from jax.sharding import PartitionSpec as P

HD = 128
BLOCK = 128
CAP = 2
CB_DEV = 8
GROUPS = 2
PARTS = 4
NEG = -1e30
EXP2_SCALE = HD**-0.5 * 1.4426950408889634
F32 = jnp.float32
BF16 = jnp.bfloat16


def remote(src, dst, send_sem, recv_sem, device):
    return pltpu.make_async_remote_copy(
        src_ref=src,
        dst_ref=dst,
        send_sem=send_sem,
        recv_sem=recv_sem,
        device_id=device,
        device_id_type=pl.DeviceIdType.MESH,
    )


def kernel(
    n, n_head, kvh, group,
    list_ref, count_ref, q_ref, kn_ref, vn_ref, ck_ref, cv_ref, w_hbm,
    out_ref,
    table, meta, meta_s, far_table, far_q, prev, qstack, sendb, recvb, acc, stat,
    part_out, part_in, stat_in, att, w_v, proj, proj16, r1, s2, r2,
    meta_ss, meta_rs, smem_s, kv_ss, kv_rs, prev_ss, prev_rs, far_ss, far_rs,
    back_ss, back_rs, w_sem, p1_ss, p1_rs, p2_ss, p2_rs,
):
    me = lax.axis_index("ctx")
    hi = lax.axis_index("head")
    half = n // GROUPS
    mypos = lax.rem(me, half)
    base = me - mypos
    mirror = lax.rem(me + half, n)
    cols = w_v.shape[2]

    def w_copy(c):
        return pltpu.make_async_copy(
            w_hbm.at[:, pl.ds(c * cols, cols)], w_v.at[c], w_sem.at[c]
        )

    barrier = pltpu.get_barrier_semaphore()
    for k in range(1, n):
        pl.semaphore_signal(
            barrier, inc=1, device_id={"ctx": lax.rem(me + k, n)},
            device_id_type=pl.DeviceIdType.MESH,
        )
    for k in range(1, n_head):
        pl.semaphore_signal(
            barrier, inc=1, device_id={"head": lax.rem(hi + k, n_head)},
            device_id_type=pl.DeviceIdType.MESH,
        )

    blk = list_ref[...]
    lane = lax.broadcasted_iota(jnp.int32, blk.shape, 1)
    head = lax.broadcasted_iota(jnp.int32, blk.shape, 0)
    used = jnp.full_like(blk, -1)
    for h in range(kvh):
        used = jnp.where((head == h) & (lane < count_ref[0, h]), blk, used)
    for o in range(n):
        mine = (used >= o * CB_DEV) & (used < (o + 1) * CB_DEV)
        first = jnp.min(jnp.where(mine, used - o * CB_DEV, CB_DEV - 1), axis=1, keepdims=True)
        last = jnp.max(jnp.where(mine, used - o * CB_DEV, 0), axis=1, keepdims=True)
        two = (last > first).astype(jnp.int32)
        table[o, 0:kvh, :] = jnp.broadcast_to(first, (kvh, 128))
        table[o, kvh : 2 * kvh, :] = jnp.broadcast_to(last, (kvh, 128))
        table[o, 2 * kvh : 3 * kvh, :] = jnp.broadcast_to(two, (kvh, 128))

    pl.semaphore_wait(barrier, n - 1 + n_head - 1)

    def meta_send(k):
        d = lax.rem(me + k, n)
        return remote(table.at[d], meta.at[me], meta_ss.at[k], meta_rs.at[me], {"ctx": d})

    def meta_recv(d):
        return remote(table.at[d], meta.at[d], meta_ss.at[0], meta_rs.at[d], {"ctx": mirror})

    for k in range(1, n):
        meta_send(k).start()
    far_copies = []
    if GROUPS == 2:
        far_copies = [
            remote(table, far_table, far_ss.at[0], far_rs.at[0], {"ctx": mirror}),
            remote(q_ref, far_q, far_ss.at[1], far_rs.at[1], {"ctx": mirror}),
        ]
    for copy in far_copies:
        copy.start()
    nxt = lax.rem(me + 1, n)
    prev_copies = [
        remote(kn_ref, prev.at[0], prev_ss.at[0], prev_rs.at[0], {"ctx": nxt}),
        remote(vn_ref, prev.at[1], prev_ss.at[1], prev_rs.at[1], {"ctx": nxt}),
    ]

    def own_smem():
        return pltpu.make_async_copy(table.at[me], meta_s.at[me], smem_s.at[me])

    own_smem().start()

    def smem_copy(d):
        return pltpu.make_async_copy(meta.at[d], meta_s.at[d], smem_s.at[d])

    def partner(k):
        place, total = 1, 0
        while place < half:
            a, b = lax.rem(mypos // place, 2), lax.rem(k // place, 2)
            total = total + place * (a + b - 2 * a * b)
            place *= 2
        return total

    def target(x, k):
        pi = partner(half - k)
        p = base + pi
        d = p if x == 0 else lax.rem(p + half, n)
        return pi, p, d

    def gather(d, dst):
        for h in range(kvh):
            for s in range(CAP):
                index = meta_s[d, s * kvh + h, 0]
                cut = slice(h * HD, (h + 1) * HD)
                dst[h, 0, s * BLOCK : (s + 1) * BLOCK, :] = ck_ref[index, :, cut]
                dst[h, 1, s * BLOCK : (s + 1) * BLOCK, :] = cv_ref[index, :, cut]

    def kv_send(x, k):
        pi, p, _ = target(x, k)
        return remote(
            sendb.at[x, pi], recvb.at[x, mypos], kv_ss.at[x, pi], kv_rs.at[x, mypos], {"ctx": p}
        )

    def kv_recv(x, k):
        pi, p, _ = target(x, k)
        return pi, remote(
            sendb.at[x, pi], recvb.at[x, pi], kv_ss.at[x, pi], kv_rs.at[x, pi], {"ctx": p}
        )

    order = list(range(GROUPS))[::-1]
    for x in order:
        def fetch(k, _, x=x):
            _, _, d = target(x, k)
            meta_recv(d).wait_recv()
            smem_copy(d).start()
            return 0

        lax.fori_loop(1, half, fetch, 0)
    if GROUPS == 2:
        meta_recv(mirror).wait_recv()
        smem_copy(mirror).start()
    for x in order:
        def give(k, _, x=x):
            pi, _, d = target(x, k)
            smem_copy(d).wait()
            gather(d, sendb.at[x, pi])
            if x == order[0]:
                kv_send(x, k).start()
            return 0

        lax.fori_loop(1, half, give, 0)

    for copy_c in range(PARTS):
        w_copy(copy_c).start()
    own_smem().wait()
    gather(me, recvb.at[0, mypos])
    if GROUPS == 2:
        smem_copy(mirror).wait()
        gather(mirror, recvb.at[1, mypos])

    width = group * BLOCK

    def stack(x, ref):
        for h in range(kvh):
            for j in range(group):
                column = (h * group + j) * HD
                qstack[x, h, j * BLOCK : (j + 1) * BLOCK, :] = ref[:, column : column + HD]

    def attend(x, h, keys, values, mask):
        scores = lax.dot_general(
            keys, qstack[x, h], (((1,), (1,)), ((), ())), preferred_element_type=F32
        )
        scores = mask(scores)
        old_max = stat[x, h : h + 1, :]
        new_max = jnp.maximum(old_max, jnp.max(scores, axis=0, keepdims=True))
        weights = jnp.exp2((scores - new_max) * EXP2_SCALE)
        fade = jnp.exp2((old_max - new_max) * EXP2_SCALE)
        total = stat[x, kvh + h : kvh + h + 1, :] * fade
        stat[x, h : h + 1, :] = new_max
        stat[x, kvh + h : kvh + h + 1, :] = total + jnp.sum(weights, axis=0, keepdims=True)
        mixture = lax.dot_general(
            values, weights.astype(BF16), (((0,), (0,)), ((), ())), preferred_element_type=F32
        )
        acc[x, h] = acc[x, h] * fade + mixture

    def attend_cache(x, pi, heads=range(kvh)):
        flags = table if x == 0 else far_table
        for h in heads:
            two = flags[base + pi, 2 * kvh + h : 2 * kvh + h + 1, :]
            two = jnp.concatenate([two] * group, axis=1)

            def mask(scores):
                return jnp.concatenate(
                    [scores[:BLOCK], jnp.where(two > 0, scores[BLOCK:], NEG)], axis=0
                )

            attend(x, h, recvb[x, pi, h, 0], recvb[x, pi, h, 1], mask)

    def attend_arrivals(x, stop):
        def step(k, _):
            pi, copy = kv_recv(x, k)
            copy.wait_recv()
            attend_cache(x, pi)
            return 0

        lax.fori_loop(1, stop, step, 0)

    stat[:, 0:kvh, :] = jnp.full((GROUPS, kvh, width), NEG, F32)
    stat[:, kvh:, :] = jnp.zeros((GROUPS, stat.shape[1] - kvh, width), F32)
    acc[...] = jnp.zeros_like(acc)
    stack(0, q_ref)

    def causal(scores):
        key = lax.broadcasted_iota(jnp.int32, scores.shape, 0)
        row = lax.broadcasted_iota(jnp.int32, scores.shape, 1) & (BLOCK - 1)
        return jnp.where(key <= row, scores, NEG)

    for h in range(kvh):
        cut = slice(h * HD, (h + 1) * HD)
        attend(0, h, kn_ref[:, cut], vn_ref[:, cut], causal)
    attend_cache(0, mypos)

    def follow(k, _):
        kv_send(1, k).wait_send()
        kv_send(0, k).start()
        return 0

    back_copies = []
    if GROUPS == 2:
        lax.fori_loop(1, half, follow, 0)
        for copy in far_copies:
            copy.wait_recv()
        stack(1, far_q)
        attend_cache(1, mypos)
        attend_arrivals(1, half - 1)
        pi, copy = kv_recv(1, half - 1)
        copy.wait_recv()
        for h in range(kvh):
            attend_cache(1, pi, [h])
            part_out[h] = acc[1, h].astype(BF16)
            copy = remote(
                part_out.at[h], part_in.at[h], back_ss.at[h], back_rs.at[h], {"ctx": mirror}
            )
            copy.start()
            back_copies.append(copy)
        copy = remote(stat.at[1], stat_in, back_ss.at[kvh], back_rs.at[kvh], {"ctx": mirror})
        copy.start()
        back_copies.append(copy)
    for copy in prev_copies:
        @pl.when(me < n - 1)
        def _(copy=copy):
            copy.start()

    @pl.when(me > 0)
    def _():
        for copy in prev_copies:
            copy.wait_recv()
        for h in range(kvh):
            cut = slice(h * HD, (h + 1) * HD)
            attend(0, h, prev[0, :, cut], prev[1, :, cut], lambda scores: scores)

    attend_arrivals(0, half)
    for copy in back_copies:
        copy.wait_recv()
    for h in range(kvh):
        own = acc[0, h]
        total = stat[0, kvh + h : kvh + h + 1, :]
        if GROUPS == 2:
            here, there = stat[0, h : h + 1, :], stat_in[h : h + 1, :]
            top = jnp.maximum(here, there)
            fade_here = jnp.exp2((here - top) * EXP2_SCALE)
            fade_there = jnp.exp2((there - top) * EXP2_SCALE)
            own = own * fade_here + part_in[h].astype(F32) * fade_there
            total = total * fade_here + stat_in[kvh + h : kvh + h + 1, :] * fade_there
        own = own / total
        for j in range(group):
            column = (h * group + j) * HD
            block = own[:, j * BLOCK : (j + 1) * BLOCK]
            att[:, column : column + HD] = block.T.astype(BF16)

    core = lax.rem(hi, 2)
    row = hi // 2
    core_peer = hi + 1 - 2 * core
    row_peer = lax.rem(hi + 2, n_head)
    piece = BLOCK // n_head

    def to_core(c):
        return remote(
            proj16.at[c, 1 - core], r1.at[c], p1_ss.at[c], p1_rs.at[c], {"head": core_peer}
        )

    def to_row(c):
        return remote(s2.at[c], r2.at[c], p2_ss.at[c], p2_rs.at[c], {"head": row_peer})

    def forward(c):
        to_core(c).wait_recv()
        s2[c] = (proj[c, core, 1 - row] + r1[c, 1 - row].astype(F32)).astype(BF16)
        to_row(c).start()

    for c in range(PARTS):
        w_copy(c).wait()
        product = jnp.dot(att[...], w_v[c], preferred_element_type=F32)
        for i in range(n_head):
            rows = product[i * piece : (i + 1) * piece]
            proj[c, i % 2, i // 2] = rows
            proj16[c, i % 2, i // 2] = rows.astype(BF16)
        to_core(c).start()
        if c > 0:
            forward(c - 1)
    forward(PARTS - 1)
    for c in range(PARTS):
        to_row(c).wait_recv()
        out_ref[:, c * cols : (c + 1) * cols] = (
            proj[c, core, row] + r1[c, row].astype(F32) + r2[c].astype(F32)
        ).astype(BF16)

    for k in range(1, n):
        meta_send(k).wait_send()
    for copy in far_copies + back_copies:
        copy.wait_send()
    for copy in prev_copies:
        @pl.when(me < n - 1)
        def _(copy=copy):
            copy.wait_send()
    def sent(k, _):
        kv_send(0, k).wait_send()
        return 0

    lax.fori_loop(1, half, sent, 0)
    for c in range(PARTS):
        to_core(c).wait_send()
        to_row(c).wait_send()


def shards(
    queries, keys_new, values_new, cache_keys, cache_values, block_list, block_count, out_weight
):
    n = lax.axis_size("ctx")
    n_head = lax.axis_size("head")
    kvh = keys_new.shape[1] // HD
    group = queries.shape[1] // keys_new.shape[1]
    half = n // GROUPS
    width = group * BLOCK
    d_in, d_out = out_weight.shape
    cols = d_out // PARTS
    piece = BLOCK // n_head
    vmem, any_space = pl.BlockSpec(memory_space=pltpu.VMEM), pl.BlockSpec(memory_space=pl.ANY)
    smem = pl.BlockSpec(memory_space=pltpu.SMEM)
    dma = pltpu.SemaphoreType.DMA
    keys_slot = CAP * BLOCK
    scratch = [
        pltpu.VMEM((n, 8, 128), jnp.int32),
        pltpu.VMEM((n, 8, 128), jnp.int32),
        pltpu.SMEM((n, 8, 128), jnp.int32),
        pltpu.VMEM((n, 8, 128), jnp.int32),
        pltpu.VMEM(queries.shape, BF16),
        pltpu.VMEM((2,) + keys_new.shape, BF16),
        pltpu.VMEM((GROUPS, kvh, width, HD), BF16),
        pltpu.VMEM((GROUPS, half, kvh, 2, keys_slot, HD), BF16),
        pltpu.VMEM((GROUPS, half, kvh, 2, keys_slot, HD), BF16),
        pltpu.VMEM((GROUPS, kvh, HD, width), F32),
        pltpu.VMEM((GROUPS, 8, width), F32),
        pltpu.VMEM((kvh, HD, width), BF16),
        pltpu.VMEM((kvh, HD, width), BF16),
        pltpu.VMEM((8, width), F32),
        pltpu.VMEM((BLOCK, d_in), BF16),
        pltpu.VMEM((PARTS, d_in, cols), BF16),
        pltpu.VMEM((PARTS, 2, n_head // 2, piece, cols), F32),
        pltpu.VMEM((PARTS, 2, n_head // 2, piece, cols), BF16),
        pltpu.VMEM((PARTS, n_head // 2, piece, cols), BF16),
        pltpu.VMEM((PARTS, piece, cols), BF16),
        pltpu.VMEM((PARTS, piece, cols), BF16),
        dma((n,)), dma((n,)), dma((n,)),
        dma((GROUPS, half)), dma((GROUPS, half)),
        dma((2,)), dma((2,)), dma((2,)), dma((2,)), dma((kvh + 1,)), dma((kvh + 1,)),
        dma((PARTS,)), dma((PARTS,)), dma((PARTS,)), dma((PARTS,)), dma((PARTS,)),
    ]
    return pl.pallas_call(
        functools.partial(kernel, n, n_head, kvh, group),
        out_shape=jax.ShapeDtypeStruct((piece, d_out), BF16),
        in_specs=[vmem, smem] + [vmem] * 5 + [any_space],
        out_specs=vmem,
        scratch_shapes=scratch,
        compiler_params=pltpu.CompilerParams(
            collective_id=0, has_side_effects=True, vmem_limit_bytes=56 * 2**20
        ),
    )(
        block_list.reshape(kvh, -1), block_count.reshape(1, kvh),
        queries, keys_new, values_new,
        cache_keys.reshape(CB_DEV, BLOCK, -1), cache_values.reshape(CB_DEV, BLOCK, -1), out_weight,
    )


def solution(mesh):
    return jax.shard_map(
        shards,
        mesh=mesh,
        in_specs=(
            P("ctx", "head"),
            P("ctx", "head"),
            P("ctx", "head"),
            P("ctx", "head"),
            P("ctx", "head"),
            P("head", "ctx", None),
            P("head", "ctx"),
            P("head", None),
        ),
        out_specs=P(("ctx", "head"), None),
        check_vma=False,
    )
```

```python
import functools

import jax
import jax.numpy as jnp
from jax import lax
from jax.experimental import pallas as pl
from jax.experimental.pallas import tpu as pltpu
from jax.sharding import PartitionSpec as P

HD = 128
BLOCK = 128
CAP = 2
CB_DEV = 8
GROUPS = 2
PARTS = 4
NEG = -1e30
EXP2_SCALE = HD**-0.5 * 1.4426950408889634
F32 = jnp.float32
BF16 = jnp.bfloat16


def remote(src, dst, send_sem, recv_sem, device):
    return pltpu.make_async_remote_copy(
        src_ref=src,
        dst_ref=dst,
        send_sem=send_sem,
        recv_sem=recv_sem,
        device_id=device,
        device_id_type=pl.DeviceIdType.MESH,
    )


def kernel(
    n, n_head, kvh, group,
    list_ref, count_ref, q_ref, kn_ref, vn_ref, ck_ref, cv_ref, w_hbm,
    out_ref,
    table, meta, meta_s, far_table, far_q, prev, qstack, sendb, recvb, acc, stat,
    part_out, part_in, stat_in, att, w_v, proj, proj16, r1, s2, r2,
    meta_ss, meta_rs, smem_s, kv_ss, kv_rs, prev_ss, prev_rs, far_ss, far_rs,
    back_ss, back_rs, w_sem, p1_ss, p1_rs, p2_ss, p2_rs,
):
    me = lax.axis_index("ctx")
    hi = lax.axis_index("head")
    half = n // GROUPS
    mypos = lax.rem(me, half)
    base = me - mypos
    mirror = lax.rem(me + half, n)
    cols = w_v.shape[2]

    def w_copy(c):
        return pltpu.make_async_copy(
            w_hbm.at[:, pl.ds(c * cols, cols)], w_v.at[c], w_sem.at[c]
        )

    barrier = pltpu.get_barrier_semaphore()
    for k in range(1, n):
        pl.semaphore_signal(
            barrier, inc=1, device_id={"ctx": lax.rem(me + k, n)},
            device_id_type=pl.DeviceIdType.MESH,
        )
    for k in range(1, n_head):
        pl.semaphore_signal(
            barrier, inc=1, device_id={"head": lax.rem(hi + k, n_head)},
            device_id_type=pl.DeviceIdType.MESH,
        )

    blk = list_ref[...]
    lane = lax.broadcasted_iota(jnp.int32, blk.shape, 1)
    head = lax.broadcasted_iota(jnp.int32, blk.shape, 0)
    used = jnp.full_like(blk, -1)
    for h in range(kvh):
        used = jnp.where((head == h) & (lane < count_ref[0, h]), blk, used)
    for o in range(n):
        mine = (used >= o * CB_DEV) & (used < (o + 1) * CB_DEV)
        first = jnp.min(jnp.where(mine, used - o * CB_DEV, CB_DEV - 1), axis=1, keepdims=True)
        last = jnp.max(jnp.where(mine, used - o * CB_DEV, 0), axis=1, keepdims=True)
        two = (last > first).astype(jnp.int32)
        table[o, 0:kvh, :] = jnp.broadcast_to(first, (kvh, 128))
        table[o, kvh : 2 * kvh, :] = jnp.broadcast_to(last, (kvh, 128))
        table[o, 2 * kvh : 3 * kvh, :] = jnp.broadcast_to(two, (kvh, 128))

    pl.semaphore_wait(barrier, n - 1 + n_head - 1)

    def meta_send(k):
        d = lax.rem(me + k, n)
        return remote(table.at[d], meta.at[me], meta_ss.at[k], meta_rs.at[me], {"ctx": d})

    def meta_recv(d):
        return remote(table.at[d], meta.at[d], meta_ss.at[0], meta_rs.at[d], {"ctx": mirror})

    for k in range(1, n):
        meta_send(k).start()
    far_copies = []
    if GROUPS == 2:
        far_copies = [
            remote(table, far_table, far_ss.at[0], far_rs.at[0], {"ctx": mirror}),
            remote(q_ref, far_q, far_ss.at[1], far_rs.at[1], {"ctx": mirror}),
        ]
    for copy in far_copies:
        copy.start()
    nxt = lax.rem(me + 1, n)
    prev_copies = [
        remote(kn_ref, prev.at[0], prev_ss.at[0], prev_rs.at[0], {"ctx": nxt}),
        remote(vn_ref, prev.at[1], prev_ss.at[1], prev_rs.at[1], {"ctx": nxt}),
    ]

    def own_smem():
        return pltpu.make_async_copy(table.at[me], meta_s.at[me], smem_s.at[me])

    own_smem().start()

    def smem_copy(d):
        return pltpu.make_async_copy(meta.at[d], meta_s.at[d], smem_s.at[d])

    def target(x, k):
        pi = lax.rem(mypos + k, half)
        p = base + pi
        d = p if x == 0 else lax.rem(p + half, n)
        return pi, p, d

    def gather(d, dst):
        for h in range(kvh):
            for s in range(CAP):
                index = meta_s[d, s * kvh + h, 0]
                cut = slice(h * HD, (h + 1) * HD)
                dst[h, 0, s * BLOCK : (s + 1) * BLOCK, :] = ck_ref[index, :, cut]
                dst[h, 1, s * BLOCK : (s + 1) * BLOCK, :] = cv_ref[index, :, cut]

    def kv_send(x, k):
        pi, p, _ = target(x, k)
        return remote(
            sendb.at[x, pi], recvb.at[x, mypos], kv_ss.at[x, pi], kv_rs.at[x, mypos], {"ctx": p}
        )

    def kv_recv(x, k):
        pi, p, _ = target(x, half - k)
        return pi, remote(
            sendb.at[x, pi], recvb.at[x, pi], kv_ss.at[x, pi], kv_rs.at[x, pi], {"ctx": p}
        )

    order = list(range(GROUPS))[::-1]
    for x in order:
        def fetch(k, _, x=x):
            _, _, d = target(x, k)
            meta_recv(d).wait_recv()
            smem_copy(d).start()
            return 0

        lax.fori_loop(1, half, fetch, 0)
    if GROUPS == 2:
        meta_recv(mirror).wait_recv()
        smem_copy(mirror).start()
    for x in order:
        def give(k, _, x=x):
            pi, _, d = target(x, k)
            smem_copy(d).wait()
            gather(d, sendb.at[x, pi])
            kv_send(x, k).start()
            return 0

        lax.fori_loop(1, half, give, 0)
        if x == order[0]:
            for copy in prev_copies:
                @pl.when(me < n - 1)
                def _(copy=copy):
                    copy.start()

    for copy_c in range(PARTS):
        w_copy(copy_c).start()
    own_smem().wait()
    gather(me, recvb.at[0, mypos])
    if GROUPS == 2:
        smem_copy(mirror).wait()
        gather(mirror, recvb.at[1, mypos])

    width = group * BLOCK

    def stack(x, ref):
        for h in range(kvh):
            for j in range(group):
                column = (h * group + j) * HD
                qstack[x, h, j * BLOCK : (j + 1) * BLOCK, :] = ref[:, column : column + HD]

    def attend(x, h, keys, values, mask):
        scores = lax.dot_general(
            keys, qstack[x, h], (((1,), (1,)), ((), ())), preferred_element_type=F32
        )
        scores = mask(scores)
        old_max = stat[x, h : h + 1, :]
        new_max = jnp.maximum(old_max, jnp.max(scores, axis=0, keepdims=True))
        weights = jnp.exp2((scores - new_max) * EXP2_SCALE)
        fade = jnp.exp2((old_max - new_max) * EXP2_SCALE)
        total = stat[x, kvh + h : kvh + h + 1, :] * fade
        stat[x, h : h + 1, :] = new_max
        stat[x, kvh + h : kvh + h + 1, :] = total + jnp.sum(weights, axis=0, keepdims=True)
        mixture = lax.dot_general(
            values, weights.astype(BF16), (((0,), (0,)), ((), ())), preferred_element_type=F32
        )
        acc[x, h] = acc[x, h] * fade + mixture

    def attend_cache(x, pi, heads=range(kvh)):
        flags = table if x == 0 else far_table
        for h in heads:
            two = flags[base + pi, 2 * kvh + h : 2 * kvh + h + 1, :]
            two = jnp.concatenate([two] * group, axis=1)

            def mask(scores):
                return jnp.concatenate(
                    [scores[:BLOCK], jnp.where(two > 0, scores[BLOCK:], NEG)], axis=0
                )

            attend(x, h, recvb[x, pi, h, 0], recvb[x, pi, h, 1], mask)

    def attend_arrivals(x, stop):
        def step(k, _):
            pi, copy = kv_recv(x, k)
            copy.wait_recv()
            attend_cache(x, pi)
            return 0

        lax.fori_loop(1, stop, step, 0)

    stat[:, 0:kvh, :] = jnp.full((GROUPS, kvh, width), NEG, F32)
    stat[:, kvh:, :] = jnp.zeros((GROUPS, stat.shape[1] - kvh, width), F32)
    acc[...] = jnp.zeros_like(acc)
    stack(0, q_ref)

    def causal(scores):
        key = lax.broadcasted_iota(jnp.int32, scores.shape, 0)
        row = lax.broadcasted_iota(jnp.int32, scores.shape, 1) & (BLOCK - 1)
        return jnp.where(key <= row, scores, NEG)

    for h in range(kvh):
        cut = slice(h * HD, (h + 1) * HD)
        attend(0, h, kn_ref[:, cut], vn_ref[:, cut], causal)
    attend_cache(0, mypos)

    back_copies = []
    if GROUPS == 2:
        for copy in far_copies:
            copy.wait_recv()
        stack(1, far_q)
        attend_cache(1, mypos)
        attend_arrivals(1, half - 1)
        pi, copy = kv_recv(1, half - 1)
        copy.wait_recv()
        for h in range(kvh):
            attend_cache(1, pi, [h])
            part_out[h] = acc[1, h].astype(BF16)
            copy = remote(
                part_out.at[h], part_in.at[h], back_ss.at[h], back_rs.at[h], {"ctx": mirror}
            )
            copy.start()
            back_copies.append(copy)
        copy = remote(stat.at[1], stat_in, back_ss.at[kvh], back_rs.at[kvh], {"ctx": mirror})
        copy.start()
        back_copies.append(copy)

    @pl.when(me > 0)
    def _():
        for copy in prev_copies:
            copy.wait_recv()
        for h in range(kvh):
            cut = slice(h * HD, (h + 1) * HD)
            attend(0, h, prev[0, :, cut], prev[1, :, cut], lambda scores: scores)

    attend_arrivals(0, half)
    for copy in back_copies:
        copy.wait_recv()
    for h in range(kvh):
        own = acc[0, h]
        total = stat[0, kvh + h : kvh + h + 1, :]
        if GROUPS == 2:
            here, there = stat[0, h : h + 1, :], stat_in[h : h + 1, :]
            top = jnp.maximum(here, there)
            fade_here = jnp.exp2((here - top) * EXP2_SCALE)
            fade_there = jnp.exp2((there - top) * EXP2_SCALE)
            own = own * fade_here + part_in[h].astype(F32) * fade_there
            total = total * fade_here + stat_in[kvh + h : kvh + h + 1, :] * fade_there
        own = own / total
        for j in range(group):
            column = (h * group + j) * HD
            block = own[:, j * BLOCK : (j + 1) * BLOCK]
            att[:, column : column + HD] = block.T.astype(BF16)

    core = lax.rem(hi, 2)
    row = hi // 2
    core_peer = hi + 1 - 2 * core
    row_peer = lax.rem(hi + 2, n_head)
    piece = BLOCK // n_head

    def to_core(c):
        return remote(
            proj16.at[c, 1 - core], r1.at[c], p1_ss.at[c], p1_rs.at[c], {"head": core_peer}
        )

    def to_row(c):
        return remote(s2.at[c], r2.at[c], p2_ss.at[c], p2_rs.at[c], {"head": row_peer})

    def forward(c):
        to_core(c).wait_recv()
        s2[c] = (proj[c, core, 1 - row] + r1[c, 1 - row].astype(F32)).astype(BF16)
        to_row(c).start()

    for c in range(PARTS):
        w_copy(c).wait()
        product = jnp.dot(att[...], w_v[c], preferred_element_type=F32)
        for i in range(n_head):
            rows = product[i * piece : (i + 1) * piece]
            proj[c, i % 2, i // 2] = rows
            proj16[c, i % 2, i // 2] = rows.astype(BF16)
        to_core(c).start()
        if c > 0:
            forward(c - 1)
    forward(PARTS - 1)
    for c in range(PARTS):
        to_row(c).wait_recv()
        out_ref[:, c * cols : (c + 1) * cols] = (
            proj[c, core, row] + r1[c, row].astype(F32) + r2[c].astype(F32)
        ).astype(BF16)

    for k in range(1, n):
        meta_send(k).wait_send()
    for copy in far_copies + back_copies:
        copy.wait_send()
    for copy in prev_copies:
        @pl.when(me < n - 1)
        def _(copy=copy):
            copy.wait_send()
    for x in range(GROUPS):
        def sent(k, _, x=x):
            kv_send(x, k).wait_send()
            return 0

        lax.fori_loop(1, half, sent, 0)
    for c in range(PARTS):
        to_core(c).wait_send()
        to_row(c).wait_send()


def shards(
    queries, keys_new, values_new, cache_keys, cache_values, block_list, block_count, out_weight
):
    n = lax.axis_size("ctx")
    n_head = lax.axis_size("head")
    kvh = keys_new.shape[1] // HD
    group = queries.shape[1] // keys_new.shape[1]
    half = n // GROUPS
    width = group * BLOCK
    d_in, d_out = out_weight.shape
    cols = d_out // PARTS
    piece = BLOCK // n_head
    vmem, any_space = pl.BlockSpec(memory_space=pltpu.VMEM), pl.BlockSpec(memory_space=pl.ANY)
    smem = pl.BlockSpec(memory_space=pltpu.SMEM)
    dma = pltpu.SemaphoreType.DMA
    keys_slot = CAP * BLOCK
    scratch = [
        pltpu.VMEM((n, 8, 128), jnp.int32),
        pltpu.VMEM((n, 8, 128), jnp.int32),
        pltpu.SMEM((n, 8, 128), jnp.int32),
        pltpu.VMEM((n, 8, 128), jnp.int32),
        pltpu.VMEM(queries.shape, BF16),
        pltpu.VMEM((2,) + keys_new.shape, BF16),
        pltpu.VMEM((GROUPS, kvh, width, HD), BF16),
        pltpu.VMEM((GROUPS, half, kvh, 2, keys_slot, HD), BF16),
        pltpu.VMEM((GROUPS, half, kvh, 2, keys_slot, HD), BF16),
        pltpu.VMEM((GROUPS, kvh, HD, width), F32),
        pltpu.VMEM((GROUPS, 8, width), F32),
        pltpu.VMEM((kvh, HD, width), BF16),
        pltpu.VMEM((kvh, HD, width), BF16),
        pltpu.VMEM((8, width), F32),
        pltpu.VMEM((BLOCK, d_in), BF16),
        pltpu.VMEM((PARTS, d_in, cols), BF16),
        pltpu.VMEM((PARTS, 2, n_head // 2, piece, cols), F32),
        pltpu.VMEM((PARTS, 2, n_head // 2, piece, cols), BF16),
        pltpu.VMEM((PARTS, n_head // 2, piece, cols), BF16),
        pltpu.VMEM((PARTS, piece, cols), BF16),
        pltpu.VMEM((PARTS, piece, cols), BF16),
        dma((n,)), dma((n,)), dma((n,)),
        dma((GROUPS, half)), dma((GROUPS, half)),
        dma((2,)), dma((2,)), dma((2,)), dma((2,)), dma((kvh + 1,)), dma((kvh + 1,)),
        dma((PARTS,)), dma((PARTS,)), dma((PARTS,)), dma((PARTS,)), dma((PARTS,)),
    ]
    return pl.pallas_call(
        functools.partial(kernel, n, n_head, kvh, group),
        out_shape=jax.ShapeDtypeStruct((piece, d_out), BF16),
        in_specs=[vmem, smem] + [vmem] * 5 + [any_space],
        out_specs=vmem,
        scratch_shapes=scratch,
        compiler_params=pltpu.CompilerParams(
            collective_id=0, has_side_effects=True, vmem_limit_bytes=56 * 2**20
        ),
    )(
        block_list.reshape(kvh, -1), block_count.reshape(1, kvh),
        queries, keys_new, values_new,
        cache_keys.reshape(CB_DEV, BLOCK, -1), cache_values.reshape(CB_DEV, BLOCK, -1), out_weight,
    )


def solution(mesh):
    return jax.shard_map(
        shards,
        mesh=mesh,
        in_specs=(
            P("ctx", "head"),
            P("ctx", "head"),
            P("ctx", "head"),
            P("ctx", "head"),
            P("ctx", "head"),
            P("head", "ctx", None),
            P("head", "ctx"),
            P("head", None),
        ),
        out_specs=P(("ctx", "head"), None),
        check_vma=False,
    )
```

```python
import functools

import jax
import jax.numpy as jnp
from jax import lax
from jax.experimental import pallas as pl
from jax.experimental.pallas import tpu as pltpu
from jax.sharding import PartitionSpec as P

HD = 128
BLOCK = 128
CAP = 2
CB_DEV = 8
GROUPS = 2
PARTS = 4
NEG = -1e30
EXP2_SCALE = HD**-0.5 * 1.4426950408889634
F32 = jnp.float32
BF16 = jnp.bfloat16


def remote(src, dst, send_sem, recv_sem, device):
    return pltpu.make_async_remote_copy(
        src_ref=src,
        dst_ref=dst,
        send_sem=send_sem,
        recv_sem=recv_sem,
        device_id=device,
        device_id_type=pl.DeviceIdType.MESH,
    )


def kernel(
    n, n_head, kvh, group,
    list_ref, count_ref, q_ref, kn_ref, vn_ref, ck_ref, cv_ref, w_hbm,
    out_ref,
    table, meta, meta_s, far_table, far_q, prev, qstack, sendb, recvb, acc, stat,
    part_out, part_in, stat_in, att, w_v, proj, proj16, r1, s2, r2,
    meta_ss, meta_rs, smem_s, kv_ss, kv_rs, prev_ss, prev_rs, far_ss, far_rs,
    back_ss, back_rs, w_sem, p1_ss, p1_rs, p2_ss, p2_rs,
):
    me = lax.axis_index("ctx")
    hi = lax.axis_index("head")
    half = n // GROUPS
    mypos = lax.rem(me, half)
    base = me - mypos
    mirror = lax.rem(me + half, n)
    cols = w_v.shape[2]
    core = lax.rem(hi, 2)
    row = hi // 2
    core_peer = hi + 1 - 2 * core
    row_peer = lax.rem(hi + 2, n_head)
    sides = (1 - row, row)
    piece = BLOCK // n_head
    rows_half = BLOCK // 2

    def w_copy(c):
        return pltpu.make_async_copy(
            w_hbm.at[:, pl.ds(c * cols, cols)], w_v.at[c], w_sem.at[c]
        )

    barrier = pltpu.get_barrier_semaphore()
    for k in range(1, n):
        pl.semaphore_signal(
            barrier, inc=1, device_id={"ctx": lax.rem(me + k, n)},
            device_id_type=pl.DeviceIdType.MESH,
        )
    for k in range(1, n_head):
        pl.semaphore_signal(
            barrier, inc=1, device_id={"head": lax.rem(hi + k, n_head)},
            device_id_type=pl.DeviceIdType.MESH,
        )

    blk = list_ref[...]
    lane = lax.broadcasted_iota(jnp.int32, blk.shape, 1)
    head = lax.broadcasted_iota(jnp.int32, blk.shape, 0)
    used = jnp.full_like(blk, -1)
    for h in range(kvh):
        used = jnp.where((head == h) & (lane < count_ref[0, h]), blk, used)
    for o in range(n):
        mine = (used >= o * CB_DEV) & (used < (o + 1) * CB_DEV)
        first = jnp.min(jnp.where(mine, used - o * CB_DEV, CB_DEV - 1), axis=1, keepdims=True)
        last = jnp.max(jnp.where(mine, used - o * CB_DEV, 0), axis=1, keepdims=True)
        two = (last > first).astype(jnp.int32)
        table[o, 0:kvh, :] = jnp.broadcast_to(first, (kvh, 128))
        table[o, kvh : 2 * kvh, :] = jnp.broadcast_to(last, (kvh, 128))
        table[o, 2 * kvh : 3 * kvh, :] = jnp.broadcast_to(two, (kvh, 128))

    pl.semaphore_wait(barrier, n - 1 + n_head - 1)

    def meta_send(k):
        d = lax.rem(me + k, n)
        return remote(table.at[d], meta.at[me], meta_ss.at[k], meta_rs.at[me], {"ctx": d})

    def meta_recv(d):
        return remote(table.at[d], meta.at[d], meta_ss.at[0], meta_rs.at[d], {"ctx": mirror})

    for k in range(1, n):
        meta_send(k).start()
    far_copies = []
    if GROUPS == 2:
        far_copies = [
            remote(table, far_table, far_ss.at[0], far_rs.at[0], {"ctx": mirror}),
            remote(q_ref, far_q, far_ss.at[1], far_rs.at[1], {"ctx": mirror}),
        ]
    for copy in far_copies:
        copy.start()
    nxt = lax.rem(me + 1, n)
    prev_copies = [
        remote(kn_ref, prev.at[0], prev_ss.at[0], prev_rs.at[0], {"ctx": nxt}),
        remote(vn_ref, prev.at[1], prev_ss.at[1], prev_rs.at[1], {"ctx": nxt}),
    ]

    for copy in prev_copies:
        @pl.when(me < n - 1)
        def _(copy=copy):
            copy.start()

    def own_smem():
        return pltpu.make_async_copy(table.at[me], meta_s.at[me], smem_s.at[me])

    own_smem().start()

    def smem_copy(d):
        return pltpu.make_async_copy(meta.at[d], meta_s.at[d], smem_s.at[d])

    def target(x, k):
        pi = lax.rem(mypos + k, half)
        p = base + pi
        d = p if x == 0 else lax.rem(p + half, n)
        return pi, p, d

    def gather(d, dst):
        for h in range(kvh):
            for s in range(CAP):
                index = meta_s[d, s * kvh + h, 0]
                cut = slice(h * HD, (h + 1) * HD)
                dst[h, 0, s * BLOCK : (s + 1) * BLOCK, :] = ck_ref[index, :, cut]
                dst[h, 1, s * BLOCK : (s + 1) * BLOCK, :] = cv_ref[index, :, cut]

    def kv_send(x, k):
        pi, p, _ = target(x, k)
        return remote(
            sendb.at[x, pi], recvb.at[x, mypos], kv_ss.at[x, pi], kv_rs.at[x, mypos], {"ctx": p}
        )

    def kv_recv(x, k):
        pi, p, _ = target(x, half - k)
        return pi, remote(
            sendb.at[x, pi], recvb.at[x, pi], kv_ss.at[x, pi], kv_rs.at[x, pi], {"ctx": p}
        )

    order = list(range(GROUPS))[::-1]
    for x in order:
        def fetch(k, _, x=x):
            _, _, d = target(x, k)
            meta_recv(d).wait_recv()
            smem_copy(d).start()
            return 0

        lax.fori_loop(1, half, fetch, 0)
    if GROUPS == 2:
        meta_recv(mirror).wait_recv()
        smem_copy(mirror).start()
    for x in order:
        def give(k, _, x=x):
            pi, _, d = target(x, k)
            smem_copy(d).wait()
            gather(d, sendb.at[x, pi])
            kv_send(x, k).start()
            return 0

        lax.fori_loop(1, half, give, 0)

    for copy_c in range(PARTS):
        w_copy(copy_c).start()
    own_smem().wait()
    gather(me, recvb.at[0, mypos])
    if GROUPS == 2:
        smem_copy(mirror).wait()
        gather(mirror, recvb.at[1, mypos])

    width = group * rows_half

    def stack(x, ref):
        for h in range(kvh):
            for j in range(group):
                column = (h * group + j) * HD
                for f in range(2):
                    qstack[x, h, f, j * rows_half : (j + 1) * rows_half, :] = ref[
                        f * rows_half : (f + 1) * rows_half, column : column + HD
                    ]

    def attend(x, h, f, keys, values, mask):
        scores = lax.dot_general(
            keys, qstack[x, h, f], (((1,), (1,)), ((), ())), preferred_element_type=F32
        )
        scores = mask(scores)
        old_max = stat[x, f, h : h + 1, :]
        new_max = jnp.maximum(old_max, jnp.max(scores, axis=0, keepdims=True))
        weights = jnp.exp2((scores - new_max) * EXP2_SCALE)
        fade = jnp.exp2((old_max - new_max) * EXP2_SCALE)
        total = stat[x, f, kvh + h : kvh + h + 1, :] * fade
        stat[x, f, h : h + 1, :] = new_max
        stat[x, f, kvh + h : kvh + h + 1, :] = total + jnp.sum(weights, axis=0, keepdims=True)
        mixture = lax.dot_general(
            values, weights.astype(BF16), (((0,), (0,)), ((), ())), preferred_element_type=F32
        )
        acc[x, h, f] = acc[x, h, f] * fade + mixture

    def attend_cache(x, pi, halves=(0, 1)):
        flags = table if x == 0 else far_table
        for f in halves:
            for h in range(kvh):
                two = flags[base + pi, 2 * kvh + h : 2 * kvh + h + 1, :]
                two = jnp.concatenate([two] * (width // 128), axis=1)

                def mask(scores, two=two):
                    return jnp.concatenate(
                        [scores[:BLOCK], jnp.where(two > 0, scores[BLOCK:], NEG)], axis=0
                    )

                attend(x, h, f, recvb[x, pi, h, 0], recvb[x, pi, h, 1], mask)

    def attend_arrivals(x, stop):
        def step(k, _):
            pi, copy = kv_recv(x, k)
            copy.wait_recv()
            attend_cache(x, pi)
            return 0

        lax.fori_loop(1, stop, step, 0)

    stat[:, :, 0:kvh, :] = jnp.full((GROUPS, 2, kvh, width), NEG, F32)
    stat[:, :, kvh:, :] = jnp.zeros((GROUPS, 2, stat.shape[2] - kvh, width), F32)
    acc[...] = jnp.zeros_like(acc)
    stack(0, q_ref)

    def causal(f, scores):
        key = lax.broadcasted_iota(jnp.int32, scores.shape, 0)
        lane = lax.broadcasted_iota(jnp.int32, scores.shape, 1)
        return jnp.where(key <= f * rows_half + (lane & (rows_half - 1)), scores, NEG)

    for h in range(kvh):
        cut = slice(h * HD, (h + 1) * HD)
        for f in range(2):
            attend(0, h, f, kn_ref[:, cut], vn_ref[:, cut], functools.partial(causal, f))
    attend_cache(0, mypos)

    back_copies = []
    if GROUPS == 2:
        for copy in far_copies:
            copy.wait_recv()
        stack(1, far_q)
        attend_cache(1, mypos)
        attend_arrivals(1, half - 1)
        pi, copy = kv_recv(1, half - 1)
        copy.wait_recv()
        for i, f in enumerate(sides):
            attend_cache(1, pi, [f])
            for h in range(kvh):
                part_out[f, h] = acc[1, h, f].astype(BF16)
            pair = [
                remote(
                    stat.at[1, f], stat_in.at[f], back_ss.at[i, 0], back_rs.at[i, 0],
                    {"ctx": mirror},
                ),
                remote(
                    part_out.at[f], part_in.at[f], back_ss.at[i, 1], back_rs.at[i, 1],
                    {"ctx": mirror},
                ),
            ]
            for copy in pair:
                copy.start()
            back_copies += pair

    @pl.when(me > 0)
    def _():
        for copy in prev_copies:
            copy.wait_recv()
        for h in range(kvh):
            cut = slice(h * HD, (h + 1) * HD)
            for f in range(2):
                attend(0, h, f, prev[0, :, cut], prev[1, :, cut], lambda scores: scores)

    attend_arrivals(0, half)

    def finish(i):
        f = sides[i]
        for copy in back_copies[2 * i : 2 * i + 2]:
            copy.wait_recv()
        for h in range(kvh):
            own = acc[0, h, f]
            total = stat[0, f, kvh + h : kvh + h + 1, :]
            if GROUPS == 2:
                here, there = stat[0, f, h : h + 1, :], stat_in[f, h : h + 1, :]
                top = jnp.maximum(here, there)
                fade_here = jnp.exp2((here - top) * EXP2_SCALE)
                fade_there = jnp.exp2((there - top) * EXP2_SCALE)
                own = own * fade_here + part_in[f, h].astype(F32) * fade_there
                total = total * fade_here + stat_in[f, kvh + h : kvh + h + 1, :] * fade_there
            turned = (own / total).T.astype(BF16)
            for j in range(group):
                column = (h * group + j) * HD
                att[i, :, column : column + HD] = turned[j * rows_half : (j + 1) * rows_half]

    def to_core(c, i):
        return remote(
            proj16.at[c, 1 - core, i], r1.at[c, i], p1_ss.at[c, i], p1_rs.at[c, i],
            {"head": core_peer},
        )

    def to_row(c):
        return remote(s2.at[c], r2.at[c], p2_ss.at[c], p2_rs.at[c], {"head": row_peer})

    def forward(c):
        to_core(c, 0).wait_recv()
        s2[c] = (proj[c, core, 0] + r1[c, 0].astype(F32)).astype(BF16)
        to_row(c).start()

    def project(c, i):
        product = jnp.dot(att[i], w_v[c], preferred_element_type=F32)
        for side in range(2):
            part = product[side * piece : (side + 1) * piece]
            proj[c, side, i] = part
            proj16[c, side, i] = part.astype(BF16)
        to_core(c, i).start()

    finish(0)
    for c in range(PARTS):
        w_copy(c).wait()
        project(c, 0)
        if c > 0:
            forward(c - 1)
    forward(PARTS - 1)
    finish(1)
    for c in range(PARTS):
        project(c, 1)
    for c in range(PARTS):
        to_core(c, 1).wait_recv()
        to_row(c).wait_recv()
        out_ref[:, c * cols : (c + 1) * cols] = (
            proj[c, core, 1] + r1[c, 1].astype(F32) + r2[c].astype(F32)
        ).astype(BF16)

    for k in range(1, n):
        meta_send(k).wait_send()
    for copy in far_copies + back_copies:
        copy.wait_send()
    for copy in prev_copies:
        @pl.when(me < n - 1)
        def _(copy=copy):
            copy.wait_send()
    for x in range(GROUPS):
        def sent(k, _, x=x):
            kv_send(x, k).wait_send()
            return 0

        lax.fori_loop(1, half, sent, 0)
    for c in range(PARTS):
        to_core(c, 0).wait_send()
        to_core(c, 1).wait_send()
        to_row(c).wait_send()


def shards(
    queries, keys_new, values_new, cache_keys, cache_values, block_list, block_count, out_weight
):
    n = lax.axis_size("ctx")
    n_head = lax.axis_size("head")
    kvh = keys_new.shape[1] // HD
    group = queries.shape[1] // keys_new.shape[1]
    half = n // GROUPS
    width = group * BLOCK // 2
    d_in, d_out = out_weight.shape
    cols = d_out // PARTS
    piece = BLOCK // n_head
    vmem, any_space = pl.BlockSpec(memory_space=pltpu.VMEM), pl.BlockSpec(memory_space=pl.ANY)
    smem = pl.BlockSpec(memory_space=pltpu.SMEM)
    dma = pltpu.SemaphoreType.DMA
    keys_slot = CAP * BLOCK
    scratch = [
        pltpu.VMEM((n, 8, 128), jnp.int32),
        pltpu.VMEM((n, 8, 128), jnp.int32),
        pltpu.SMEM((n, 8, 128), jnp.int32),
        pltpu.VMEM((n, 8, 128), jnp.int32),
        pltpu.VMEM(queries.shape, BF16),
        pltpu.VMEM((2,) + keys_new.shape, BF16),
        pltpu.VMEM((GROUPS, kvh, 2, width, HD), BF16),
        pltpu.VMEM((GROUPS, half, kvh, 2, keys_slot, HD), BF16),
        pltpu.VMEM((GROUPS, half, kvh, 2, keys_slot, HD), BF16),
        pltpu.VMEM((GROUPS, kvh, 2, HD, width), F32),
        pltpu.VMEM((GROUPS, 2, 8, width), F32),
        pltpu.VMEM((2, kvh, HD, width), BF16),
        pltpu.VMEM((2, kvh, HD, width), BF16),
        pltpu.VMEM((2, 8, width), F32),
        pltpu.VMEM((2, BLOCK // 2, d_in), BF16),
        pltpu.VMEM((PARTS, d_in, cols), BF16),
        pltpu.VMEM((PARTS, 2, n_head // 2, piece, cols), F32),
        pltpu.VMEM((PARTS, 2, n_head // 2, piece, cols), BF16),
        pltpu.VMEM((PARTS, n_head // 2, piece, cols), BF16),
        pltpu.VMEM((PARTS, piece, cols), BF16),
        pltpu.VMEM((PARTS, piece, cols), BF16),
        dma((n,)), dma((n,)), dma((n,)),
        dma((GROUPS, half)), dma((GROUPS, half)),
        dma((2,)), dma((2,)), dma((2,)), dma((2,)), dma((2, 2)), dma((2, 2)),
        dma((PARTS,)), dma((PARTS, 2)), dma((PARTS, 2)), dma((PARTS,)), dma((PARTS,)),
    ]
    return pl.pallas_call(
        functools.partial(kernel, n, n_head, kvh, group),
        out_shape=jax.ShapeDtypeStruct((piece, d_out), BF16),
        in_specs=[vmem, smem] + [vmem] * 5 + [any_space],
        out_specs=vmem,
        scratch_shapes=scratch,
        compiler_params=pltpu.CompilerParams(
            collective_id=0, has_side_effects=True, vmem_limit_bytes=56 * 2**20
        ),
    )(
        block_list.reshape(kvh, -1), block_count.reshape(1, kvh),
        queries, keys_new, values_new,
        cache_keys.reshape(CB_DEV, BLOCK, -1), cache_values.reshape(CB_DEV, BLOCK, -1), out_weight,
    )


def solution(mesh):
    return jax.shard_map(
        shards,
        mesh=mesh,
        in_specs=(
            P("ctx", "head"),
            P("ctx", "head"),
            P("ctx", "head"),
            P("ctx", "head"),
            P("ctx", "head"),
            P("head", "ctx", None),
            P("head", "ctx"),
            P("head", None),
        ),
        out_specs=P(("ctx", "head"), None),
        check_vma=False,
    )
```

```python
import functools

import jax
import jax.numpy as jnp
from jax import lax
from jax.experimental import pallas as pl
from jax.experimental.pallas import tpu as pltpu
from jax.sharding import PartitionSpec as P

HD = 128
BLOCK = 128
CAP = 2
CB_DEV = 8
GROUPS = 2
PARTS = 4
NEG = -1e30
EXP2_SCALE = HD**-0.5 * 1.4426950408889634
F32 = jnp.float32
BF16 = jnp.bfloat16


def remote(src, dst, send_sem, recv_sem, device):
    return pltpu.make_async_remote_copy(
        src_ref=src,
        dst_ref=dst,
        send_sem=send_sem,
        recv_sem=recv_sem,
        device_id=device,
        device_id_type=pl.DeviceIdType.MESH,
    )


def kernel(
    n, n_head, kvh, group,
    list_ref, count_ref, q_ref, kn_ref, vn_ref, ck_ref, cv_ref, w_hbm,
    out_ref,
    table, meta, meta_s, far_table, far_q, prev, qstack, sendb, recvb, acc, stat,
    part_out, part_in, stat_in, att, w_v, proj, proj16, r1, s2, r2,
    meta_ss, meta_rs, smem_s, kv_ss, kv_rs, prev_ss, prev_rs, far_ss, far_rs,
    back_ss, back_rs, w_sem, p1_ss, p1_rs, p2_ss, p2_rs,
):
    me = lax.axis_index("ctx")
    hi = lax.axis_index("head")
    half = n // GROUPS
    mypos = lax.rem(me, half)
    base = me - mypos
    mirror = lax.rem(me + half, n)
    cols = w_v.shape[2]
    core = lax.rem(hi, 2)
    row = hi // 2
    core_peer = hi + 1 - 2 * core
    row_peer = lax.rem(hi + 2, n_head)
    sides = (1 - row, row)
    piece = BLOCK // n_head
    rows_half = BLOCK // 2

    def w_copy(c):
        return pltpu.make_async_copy(
            w_hbm.at[:, pl.ds(c * cols, cols)], w_v.at[c], w_sem.at[c]
        )

    barrier = pltpu.get_barrier_semaphore()
    for k in range(1, n):
        pl.semaphore_signal(
            barrier, inc=1, device_id={"ctx": lax.rem(me + k, n)},
            device_id_type=pl.DeviceIdType.MESH,
        )
    for k in range(1, n_head):
        pl.semaphore_signal(
            barrier, inc=1, device_id={"head": lax.rem(hi + k, n_head)},
            device_id_type=pl.DeviceIdType.MESH,
        )

    blk = list_ref[...]
    lane = lax.broadcasted_iota(jnp.int32, blk.shape, 1)
    head = lax.broadcasted_iota(jnp.int32, blk.shape, 0)
    used = jnp.full_like(blk, -1)
    for h in range(kvh):
        used = jnp.where((head == h) & (lane < count_ref[0, h]), blk, used)
    for o in range(n):
        mine = (used >= o * CB_DEV) & (used < (o + 1) * CB_DEV)
        first = jnp.min(jnp.where(mine, used - o * CB_DEV, CB_DEV - 1), axis=1, keepdims=True)
        last = jnp.max(jnp.where(mine, used - o * CB_DEV, 0), axis=1, keepdims=True)
        two = (last > first).astype(jnp.int32)
        table[o, 0:kvh, :] = jnp.broadcast_to(first, (kvh, 128))
        table[o, kvh : 2 * kvh, :] = jnp.broadcast_to(last, (kvh, 128))
        table[o, 2 * kvh : 3 * kvh, :] = jnp.broadcast_to(two, (kvh, 128))

    pl.semaphore_wait(barrier, n - 1 + n_head - 1)

    def meta_send(k):
        d = lax.rem(me + k, n)
        return remote(table.at[d], meta.at[me], meta_ss.at[k], meta_rs.at[me], {"ctx": d})

    def meta_recv(d):
        return remote(table.at[d], meta.at[d], meta_ss.at[0], meta_rs.at[d], {"ctx": mirror})

    for k in range(1, n):
        meta_send(k).start()
    far_copies = []
    if GROUPS == 2:
        far_copies = [
            remote(table, far_table, far_ss.at[0], far_rs.at[0], {"ctx": mirror}),
            remote(q_ref, far_q, far_ss.at[1], far_rs.at[1], {"ctx": mirror}),
        ]
    for copy in far_copies:
        copy.start()
    nxt = lax.rem(me + 1, n)
    prev_copies = [
        remote(kn_ref, prev.at[0], prev_ss.at[0], prev_rs.at[0], {"ctx": nxt}),
        remote(vn_ref, prev.at[1], prev_ss.at[1], prev_rs.at[1], {"ctx": nxt}),
    ]

    def own_smem():
        return pltpu.make_async_copy(table.at[me], meta_s.at[me], smem_s.at[me])

    own_smem().start()

    def smem_copy(d):
        return pltpu.make_async_copy(meta.at[d], meta_s.at[d], smem_s.at[d])

    def partner(k):
        place, total = 1, 0
        while place < half:
            a, b = lax.rem(mypos // place, 2), lax.rem(k // place, 2)
            total = total + place * (a + b - 2 * a * b)
            place *= 2
        return total

    def target(x, k):
        pi = partner(lax.rem(half - k, half))
        p = base + pi
        d = p if x == 0 else lax.rem(p + half, n)
        return pi, p, d

    def gather(d, dst):
        for h in range(kvh):
            for s in range(CAP):
                index = meta_s[d, s * kvh + h, 0]
                cut = slice(h * HD, (h + 1) * HD)
                dst[h, 0, s * BLOCK : (s + 1) * BLOCK, :] = ck_ref[index, :, cut]
                dst[h, 1, s * BLOCK : (s + 1) * BLOCK, :] = cv_ref[index, :, cut]

    def kv_send(x, k):
        pi, p, _ = target(x, k)
        return remote(
            sendb.at[x, pi], recvb.at[x, mypos], kv_ss.at[x, pi], kv_rs.at[x, mypos], {"ctx": p}
        )

    def kv_recv(x, k):
        pi, p, _ = target(x, k)
        return pi, remote(
            sendb.at[x, pi], recvb.at[x, pi], kv_ss.at[x, pi], kv_rs.at[x, pi], {"ctx": p}
        )

    order = list(range(GROUPS))[::-1]
    for x in order:
        def fetch(k, _, x=x):
            _, _, d = target(x, k)
            meta_recv(d).wait_recv()
            smem_copy(d).start()
            return 0

        lax.fori_loop(1, half, fetch, 0)
    if GROUPS == 2:
        meta_recv(mirror).wait_recv()
        smem_copy(mirror).start()
    for x in order:
        def give(k, _, x=x):
            pi, _, d = target(x, k)
            smem_copy(d).wait()
            gather(d, sendb.at[x, pi])
            kv_send(x, k).start()
            return 0

        lax.fori_loop(1, half, give, 0)
        if x == order[0]:
            for copy in prev_copies:
                @pl.when(me < n - 1)
                def _(copy=copy):
                    copy.start()

    for copy_c in range(PARTS):
        w_copy(copy_c).start()
    own_smem().wait()
    gather(me, recvb.at[0, mypos])
    if GROUPS == 2:
        smem_copy(mirror).wait()
        gather(mirror, recvb.at[1, mypos])

    width = group * rows_half

    def stack(x, ref):
        for h in range(kvh):
            for j in range(group):
                column = (h * group + j) * HD
                for f in range(2):
                    qstack[x, h, f, j * rows_half : (j + 1) * rows_half, :] = ref[
                        f * rows_half : (f + 1) * rows_half, column : column + HD
                    ]

    def attend(x, h, f, keys, values, mask):
        scores = lax.dot_general(
            keys, qstack[x, h, f], (((1,), (1,)), ((), ())), preferred_element_type=F32
        )
        scores = mask(scores)
        old_max = stat[x, f, h : h + 1, :]
        new_max = jnp.maximum(old_max, jnp.max(scores, axis=0, keepdims=True))
        weights = jnp.exp2((scores - new_max) * EXP2_SCALE)
        fade = jnp.exp2((old_max - new_max) * EXP2_SCALE)
        total = stat[x, f, kvh + h : kvh + h + 1, :] * fade
        stat[x, f, h : h + 1, :] = new_max
        stat[x, f, kvh + h : kvh + h + 1, :] = total + jnp.sum(weights, axis=0, keepdims=True)
        mixture = lax.dot_general(
            values, weights.astype(BF16), (((0,), (0,)), ((), ())), preferred_element_type=F32
        )
        acc[x, h, f] = acc[x, h, f] * fade + mixture

    def attend_cache(x, pi, halves=(0, 1)):
        flags = table if x == 0 else far_table
        for f in halves:
            for h in range(kvh):
                two = flags[base + pi, 2 * kvh + h : 2 * kvh + h + 1, :]
                two = jnp.concatenate([two] * (width // 128), axis=1)

                def mask(scores, two=two):
                    return jnp.concatenate(
                        [scores[:BLOCK], jnp.where(two > 0, scores[BLOCK:], NEG)], axis=0
                    )

                attend(x, h, f, recvb[x, pi, h, 0], recvb[x, pi, h, 1], mask)

    def attend_arrivals(x, stop):
        def step(k, _):
            pi, copy = kv_recv(x, k)
            copy.wait_recv()
            attend_cache(x, pi)
            return 0

        lax.fori_loop(1, stop, step, 0)

    stat[:, :, 0:kvh, :] = jnp.full((GROUPS, 2, kvh, width), NEG, F32)
    stat[:, :, kvh:, :] = jnp.zeros((GROUPS, 2, stat.shape[2] - kvh, width), F32)
    acc[...] = jnp.zeros_like(acc)
    stack(0, q_ref)

    def causal(f, scores):
        key = lax.broadcasted_iota(jnp.int32, scores.shape, 0)
        lane = lax.broadcasted_iota(jnp.int32, scores.shape, 1)
        return jnp.where(key <= f * rows_half + (lane & (rows_half - 1)), scores, NEG)

    for h in range(kvh):
        cut = slice(h * HD, (h + 1) * HD)
        for f in range(2):
            attend(0, h, f, kn_ref[:, cut], vn_ref[:, cut], functools.partial(causal, f))
    attend_cache(0, mypos)

    back_copies = []
    if GROUPS == 2:
        for copy in far_copies:
            copy.wait_recv()
        stack(1, far_q)
        attend_cache(1, mypos)
        attend_arrivals(1, half - 1)
        pi, copy = kv_recv(1, half - 1)
        copy.wait_recv()
        for i, f in enumerate(sides):
            attend_cache(1, pi, [f])
            for h in range(kvh):
                part_out[f, h] = acc[1, h, f].astype(BF16)
            pair = [
                remote(
                    stat.at[1, f], stat_in.at[f], back_ss.at[i, 0], back_rs.at[i, 0],
                    {"ctx": mirror},
                ),
                remote(
                    part_out.at[f], part_in.at[f], back_ss.at[i, 1], back_rs.at[i, 1],
                    {"ctx": mirror},
                ),
            ]
            for copy in pair:
                copy.start()
            back_copies += pair

    @pl.when(me > 0)
    def _():
        for copy in prev_copies:
            copy.wait_recv()
        for h in range(kvh):
            cut = slice(h * HD, (h + 1) * HD)
            for f in range(2):
                attend(0, h, f, prev[0, :, cut], prev[1, :, cut], lambda scores: scores)

    attend_arrivals(0, half)

    def finish(i):
        f = sides[i]
        for copy in back_copies[2 * i : 2 * i + 2]:
            copy.wait_recv()
        for h in range(kvh):
            own = acc[0, h, f]
            total = stat[0, f, kvh + h : kvh + h + 1, :]
            if GROUPS == 2:
                here, there = stat[0, f, h : h + 1, :], stat_in[f, h : h + 1, :]
                top = jnp.maximum(here, there)
                fade_here = jnp.exp2((here - top) * EXP2_SCALE)
                fade_there = jnp.exp2((there - top) * EXP2_SCALE)
                own = own * fade_here + part_in[f, h].astype(F32) * fade_there
                total = total * fade_here + stat_in[f, kvh + h : kvh + h + 1, :] * fade_there
            turned = (own / total).T.astype(BF16)
            for j in range(group):
                column = (h * group + j) * HD
                att[i, :, column : column + HD] = turned[j * rows_half : (j + 1) * rows_half]

    def to_core(c, i):
        return remote(
            proj16.at[c, 1 - core, i], r1.at[c, i], p1_ss.at[c, i], p1_rs.at[c, i],
            {"head": core_peer},
        )

    def to_row(c):
        return remote(s2.at[c], r2.at[c], p2_ss.at[c], p2_rs.at[c], {"head": row_peer})

    def forward(c):
        to_core(c, 0).wait_recv()
        s2[c] = (proj[c, core, 0] + r1[c, 0].astype(F32)).astype(BF16)
        to_row(c).start()

    def project(c, i):
        product = jnp.dot(att[i], w_v[c], preferred_element_type=F32)
        for side in range(2):
            part = product[side * piece : (side + 1) * piece]
            proj[c, side, i] = part
            proj16[c, side, i] = part.astype(BF16)
        to_core(c, i).start()

    finish(0)
    for c in range(PARTS):
        w_copy(c).wait()
        project(c, 0)
        if c > 0:
            forward(c - 1)
    forward(PARTS - 1)
    finish(1)
    for c in range(PARTS):
        project(c, 1)
    for c in range(PARTS):
        to_core(c, 1).wait_recv()
        to_row(c).wait_recv()
        out_ref[:, c * cols : (c + 1) * cols] = (
            proj[c, core, 1] + r1[c, 1].astype(F32) + r2[c].astype(F32)
        ).astype(BF16)

    for k in range(1, n):
        meta_send(k).wait_send()
    for copy in far_copies + back_copies:
        copy.wait_send()
    for copy in prev_copies:
        @pl.when(me < n - 1)
        def _(copy=copy):
            copy.wait_send()
    for x in range(GROUPS):
        def sent(k, _, x=x):
            kv_send(x, k).wait_send()
            return 0

        lax.fori_loop(1, half, sent, 0)
    for c in range(PARTS):
        to_core(c, 0).wait_send()
        to_core(c, 1).wait_send()
        to_row(c).wait_send()


def shards(
    queries, keys_new, values_new, cache_keys, cache_values, block_list, block_count, out_weight
):
    n = lax.axis_size("ctx")
    n_head = lax.axis_size("head")
    kvh = keys_new.shape[1] // HD
    group = queries.shape[1] // keys_new.shape[1]
    half = n // GROUPS
    width = group * BLOCK // 2
    d_in, d_out = out_weight.shape
    cols = d_out // PARTS
    piece = BLOCK // n_head
    vmem, any_space = pl.BlockSpec(memory_space=pltpu.VMEM), pl.BlockSpec(memory_space=pl.ANY)
    smem = pl.BlockSpec(memory_space=pltpu.SMEM)
    dma = pltpu.SemaphoreType.DMA
    keys_slot = CAP * BLOCK
    scratch = [
        pltpu.VMEM((n, 8, 128), jnp.int32),
        pltpu.VMEM((n, 8, 128), jnp.int32),
        pltpu.SMEM((n, 8, 128), jnp.int32),
        pltpu.VMEM((n, 8, 128), jnp.int32),
        pltpu.VMEM(queries.shape, BF16),
        pltpu.VMEM((2,) + keys_new.shape, BF16),
        pltpu.VMEM((GROUPS, kvh, 2, width, HD), BF16),
        pltpu.VMEM((GROUPS, half, kvh, 2, keys_slot, HD), BF16),
        pltpu.VMEM((GROUPS, half, kvh, 2, keys_slot, HD), BF16),
        pltpu.VMEM((GROUPS, kvh, 2, HD, width), F32),
        pltpu.VMEM((GROUPS, 2, 8, width), F32),
        pltpu.VMEM((2, kvh, HD, width), BF16),
        pltpu.VMEM((2, kvh, HD, width), BF16),
        pltpu.VMEM((2, 8, width), F32),
        pltpu.VMEM((2, BLOCK // 2, d_in), BF16),
        pltpu.VMEM((PARTS, d_in, cols), BF16),
        pltpu.VMEM((PARTS, 2, n_head // 2, piece, cols), F32),
        pltpu.VMEM((PARTS, 2, n_head // 2, piece, cols), BF16),
        pltpu.VMEM((PARTS, n_head // 2, piece, cols), BF16),
        pltpu.VMEM((PARTS, piece, cols), BF16),
        pltpu.VMEM((PARTS, piece, cols), BF16),
        dma((n,)), dma((n,)), dma((n,)),
        dma((GROUPS, half)), dma((GROUPS, half)),
        dma((2,)), dma((2,)), dma((2,)), dma((2,)), dma((2, 2)), dma((2, 2)),
        dma((PARTS,)), dma((PARTS, 2)), dma((PARTS, 2)), dma((PARTS,)), dma((PARTS,)),
    ]
    return pl.pallas_call(
        functools.partial(kernel, n, n_head, kvh, group),
        out_shape=jax.ShapeDtypeStruct((piece, d_out), BF16),
        in_specs=[vmem, smem] + [vmem] * 5 + [any_space],
        out_specs=vmem,
        scratch_shapes=scratch,
        compiler_params=pltpu.CompilerParams(
            collective_id=0, has_side_effects=True, vmem_limit_bytes=56 * 2**20
        ),
    )(
        block_list.reshape(kvh, -1), block_count.reshape(1, kvh),
        queries, keys_new, values_new,
        cache_keys.reshape(CB_DEV, BLOCK, -1), cache_values.reshape(CB_DEV, BLOCK, -1), out_weight,
    )


def solution(mesh):
    return jax.shard_map(
        shards,
        mesh=mesh,
        in_specs=(
            P("ctx", "head"),
            P("ctx", "head"),
            P("ctx", "head"),
            P("ctx", "head"),
            P("ctx", "head"),
            P("head", "ctx", None),
            P("head", "ctx"),
            P("head", None),
        ),
        out_specs=P(("ctx", "head"), None),
        check_vma=False,
    )
```

```python
import functools

import jax
import jax.numpy as jnp
from jax import lax
from jax.experimental import pallas as pl
from jax.experimental.pallas import tpu as pltpu
from jax.sharding import PartitionSpec as P

HD = 128
BLOCK = 128
CAP = 2
CB_DEV = 8
GROUPS = 2
PARTS = 4
NEG = -1e30
EXP2_SCALE = HD**-0.5 * 1.4426950408889634
F32 = jnp.float32
BF16 = jnp.bfloat16


def remote(src, dst, send_sem, recv_sem, device):
    return pltpu.make_async_remote_copy(
        src_ref=src,
        dst_ref=dst,
        send_sem=send_sem,
        recv_sem=recv_sem,
        device_id=device,
        device_id_type=pl.DeviceIdType.MESH,
    )


def kernel(
    n, n_head, kvh, group,
    list_ref, count_ref, q_ref, kn_ref, vn_ref, ck_ref, cv_ref, w_hbm,
    out_ref,
    table, meta, meta_s, far_table, far_q, prev, qstack, sendb, recvb, acc, stat,
    part_out, part_in, stat_in, att, w_v, proj, proj16, r1, s2, r2,
    meta_ss, meta_rs, smem_s, kv_ss, kv_rs, prev_ss, prev_rs, far_ss, far_rs,
    back_ss, back_rs, w_sem, p1_ss, p1_rs, p2_ss, p2_rs,
):
    me = lax.axis_index("ctx")
    hi = lax.axis_index("head")
    half = n // GROUPS
    mypos = lax.rem(me, half)
    base = me - mypos
    mirror = lax.rem(me + half, n)
    cols = w_v.shape[2]
    core = lax.rem(hi, 2)
    row = hi // 2
    core_peer = hi + 1 - 2 * core
    row_peer = lax.rem(hi + 2, n_head)
    sides = (1 - row, row)
    piece = BLOCK // n_head
    rows_half = BLOCK // 2

    def w_copy(c):
        return pltpu.make_async_copy(
            w_hbm.at[:, pl.ds(c * cols, cols)], w_v.at[c], w_sem.at[c]
        )

    barrier = pltpu.get_barrier_semaphore()
    for k in range(1, n):
        pl.semaphore_signal(
            barrier, inc=1, device_id={"ctx": lax.rem(me + k, n)},
            device_id_type=pl.DeviceIdType.MESH,
        )
    for k in range(1, n_head):
        pl.semaphore_signal(
            barrier, inc=1, device_id={"head": lax.rem(hi + k, n_head)},
            device_id_type=pl.DeviceIdType.MESH,
        )

    blk = list_ref[...]
    lane = lax.broadcasted_iota(jnp.int32, blk.shape, 1)
    head = lax.broadcasted_iota(jnp.int32, blk.shape, 0)
    used = jnp.full_like(blk, -1)
    for h in range(kvh):
        used = jnp.where((head == h) & (lane < count_ref[0, h]), blk, used)
    for o in range(n):
        mine = (used >= o * CB_DEV) & (used < (o + 1) * CB_DEV)
        first = jnp.min(jnp.where(mine, used - o * CB_DEV, CB_DEV - 1), axis=1, keepdims=True)
        last = jnp.max(jnp.where(mine, used - o * CB_DEV, 0), axis=1, keepdims=True)
        two = (last > first).astype(jnp.int32)
        table[o, 0:kvh, :] = jnp.broadcast_to(first, (kvh, 128))
        table[o, kvh : 2 * kvh, :] = jnp.broadcast_to(last, (kvh, 128))
        table[o, 2 * kvh : 3 * kvh, :] = jnp.broadcast_to(two, (kvh, 128))

    pl.semaphore_wait(barrier, n - 1 + n_head - 1)

    def meta_send(k):
        d = lax.rem(me + k, n)
        return remote(table.at[d], meta.at[me], meta_ss.at[k], meta_rs.at[me], {"ctx": d})

    def meta_recv(d):
        return remote(table.at[d], meta.at[d], meta_ss.at[0], meta_rs.at[d], {"ctx": mirror})

    for k in range(1, n):
        meta_send(k).start()
    far_copies = []
    if GROUPS == 2:
        far_copies = [
            remote(table, far_table, far_ss.at[0], far_rs.at[0], {"ctx": mirror}),
            remote(q_ref, far_q, far_ss.at[1], far_rs.at[1], {"ctx": mirror}),
        ]
    for copy in far_copies:
        copy.start()
    nxt = lax.rem(me + 1, n)
    prev_copies = [
        remote(kn_ref, prev.at[0], prev_ss.at[0], prev_rs.at[0], {"ctx": nxt}),
        remote(vn_ref, prev.at[1], prev_ss.at[1], prev_rs.at[1], {"ctx": nxt}),
    ]

    def own_smem():
        return pltpu.make_async_copy(table.at[me], meta_s.at[me], smem_s.at[me])

    own_smem().start()

    def smem_copy(d):
        return pltpu.make_async_copy(meta.at[d], meta_s.at[d], smem_s.at[d])

    def partner(k):
        place, total = 1, 0
        while place < half:
            a, b = lax.rem(mypos // place, 2), lax.rem(k // place, 2)
            total = total + place * (a + b - 2 * a * b)
            place *= 2
        return total

    def target(x, k):
        pi = partner(lax.rem(half - k, half))
        p = base + pi
        d = p if x == 0 else lax.rem(p + half, n)
        return pi, p, d

    def gather(d, dst):
        for h in range(kvh):
            for s in range(CAP):
                index = meta_s[d, s * kvh + h, 0]
                cut = slice(h * HD, (h + 1) * HD)
                dst[h, 0, s * BLOCK : (s + 1) * BLOCK, :] = ck_ref[index, :, cut]
                dst[h, 1, s * BLOCK : (s + 1) * BLOCK, :] = cv_ref[index, :, cut]

    half_of = me // half
    top = mypos // (half // 2)
    inner = half_of * (1 - top) + (1 - half_of) * top

    def kv_send(x, k):
        pi, p, d = target(x, k)
        direct = x * inner * lax.div(half - k, half // 2)
        return remote(
            sendb.at[x, pi], recvb.at[x + direct, mypos],
            kv_ss.at[x, pi], kv_rs.at[x + direct, mypos], {"ctx": p + direct * (d - p)},
        )

    def kv_recv(x, k):
        pi, p, _ = target(0, k)
        return pi, remote(
            sendb.at[0, pi], recvb.at[x, pi], kv_ss.at[0, pi], kv_rs.at[x, pi], {"ctx": p}
        )

    order = list(range(GROUPS))[::-1]
    for x in order:
        def fetch(k, _, x=x):
            _, _, d = target(x, k)
            meta_recv(d).wait_recv()
            smem_copy(d).start()
            return 0

        lax.fori_loop(1, half, fetch, 0)
    if GROUPS == 2:
        meta_recv(mirror).wait_recv()
        smem_copy(mirror).start()
    for x in order:
        def give(k, _, x=x):
            pi, _, d = target(x, k)
            smem_copy(d).wait()
            gather(d, sendb.at[x, pi])
            kv_send(x, k).start()
            return 0

        lax.fori_loop(1, half, give, 0)
        if x == order[0]:
            for copy in prev_copies:
                @pl.when(me < n - 1)
                def _(copy=copy):
                    copy.start()

    for copy_c in range(PARTS):
        w_copy(copy_c).start()
    own_smem().wait()
    gather(me, recvb.at[0, mypos])
    if GROUPS == 2:
        smem_copy(mirror).wait()
        gather(mirror, recvb.at[1, mypos])

    width = group * rows_half

    def stack(x, ref):
        for h in range(kvh):
            for j in range(group):
                column = (h * group + j) * HD
                for f in range(2):
                    qstack[x, h, f, j * rows_half : (j + 1) * rows_half, :] = ref[
                        f * rows_half : (f + 1) * rows_half, column : column + HD
                    ]

    def attend(x, h, f, keys, values, mask):
        scores = lax.dot_general(
            keys, qstack[x, h, f], (((1,), (1,)), ((), ())), preferred_element_type=F32
        )
        scores = mask(scores)
        old_max = stat[x, f, h : h + 1, :]
        new_max = jnp.maximum(old_max, jnp.max(scores, axis=0, keepdims=True))
        weights = jnp.exp2((scores - new_max) * EXP2_SCALE)
        fade = jnp.exp2((old_max - new_max) * EXP2_SCALE)
        total = stat[x, f, kvh + h : kvh + h + 1, :] * fade
        stat[x, f, h : h + 1, :] = new_max
        stat[x, f, kvh + h : kvh + h + 1, :] = total + jnp.sum(weights, axis=0, keepdims=True)
        mixture = lax.dot_general(
            values, weights.astype(BF16), (((0,), (0,)), ((), ())), preferred_element_type=F32
        )
        acc[x, h, f] = acc[x, h, f] * fade + mixture

    def attend_cache(x, pi, halves=(0, 1)):
        flags = far_table if x == 1 else table
        owner = lax.rem(base + half, n) + pi if x == 2 else base + pi
        for f in halves:
            for h in range(kvh):
                two = flags[owner, 2 * kvh + h : 2 * kvh + h + 1, :]
                two = jnp.concatenate([two] * (width // 128), axis=1)

                def mask(scores, two=two):
                    return jnp.concatenate(
                        [scores[:BLOCK], jnp.where(two > 0, scores[BLOCK:], NEG)], axis=0
                    )

                attend(x % 2, h, f, recvb[x, pi, h, 0], recvb[x, pi, h, 1], mask)

    def attend_arrivals(x, first, stop):
        def step(k, _):
            pi, copy = kv_recv(x, k)
            copy.wait_recv()
            attend_cache(x, pi)
            return 0

        lax.fori_loop(first, stop, step, 0)

    stat[:, :, 0:kvh, :] = jnp.full((GROUPS, 2, kvh, width), NEG, F32)
    stat[:, :, kvh:, :] = jnp.zeros((GROUPS, 2, stat.shape[2] - kvh, width), F32)
    acc[...] = jnp.zeros_like(acc)
    stack(0, q_ref)

    def causal(f, scores):
        key = lax.broadcasted_iota(jnp.int32, scores.shape, 0)
        lane = lax.broadcasted_iota(jnp.int32, scores.shape, 1)
        return jnp.where(key <= f * rows_half + (lane & (rows_half - 1)), scores, NEG)

    for h in range(kvh):
        cut = slice(h * HD, (h + 1) * HD)
        for f in range(2):
            attend(0, h, f, kn_ref[:, cut], vn_ref[:, cut], functools.partial(causal, f))
    attend_cache(0, mypos)

    back_copies = []
    if GROUPS == 2:
        for copy in far_copies:
            copy.wait_recv()
        stack(1, far_q)
        attend_cache(1, mypos)

        @pl.when(inner == 1)
        def _():
            attend_arrivals(1, 1, half // 2 + 1)

        attend_arrivals(1, half // 2 + 1, half - 1)
        pi, copy = kv_recv(1, half - 1)
        copy.wait_recv()
        for i, f in enumerate(sides):
            attend_cache(1, pi, [f])
            for h in range(kvh):
                part_out[f, h] = acc[1, h, f].astype(BF16)
            pair = [
                remote(
                    stat.at[1, f], stat_in.at[f], back_ss.at[i, 0], back_rs.at[i, 0],
                    {"ctx": mirror},
                ),
                remote(
                    part_out.at[f], part_in.at[f], back_ss.at[i, 1], back_rs.at[i, 1],
                    {"ctx": mirror},
                ),
            ]
            for copy in pair:
                copy.start()
            back_copies += pair

    @pl.when(me > 0)
    def _():
        for copy in prev_copies:
            copy.wait_recv()
        for h in range(kvh):
            cut = slice(h * HD, (h + 1) * HD)
            for f in range(2):
                attend(0, h, f, prev[0, :, cut], prev[1, :, cut], lambda scores: scores)

    if GROUPS == 2:
        @pl.when(inner == 1)
        def _():
            attend_arrivals(2, 1, half // 2 + 1)

    attend_arrivals(0, 1, half)

    def finish(i):
        f = sides[i]
        for copy in back_copies[2 * i : 2 * i + 2]:
            copy.wait_recv()
        for h in range(kvh):
            own = acc[0, h, f]
            total = stat[0, f, kvh + h : kvh + h + 1, :]
            if GROUPS == 2:
                here, there = stat[0, f, h : h + 1, :], stat_in[f, h : h + 1, :]
                top = jnp.maximum(here, there)
                fade_here = jnp.exp2((here - top) * EXP2_SCALE)
                fade_there = jnp.exp2((there - top) * EXP2_SCALE)
                own = own * fade_here + part_in[f, h].astype(F32) * fade_there
                total = total * fade_here + stat_in[f, kvh + h : kvh + h + 1, :] * fade_there
            turned = (own / total).T.astype(BF16)
            for j in range(group):
                column = (h * group + j) * HD
                att[i, :, column : column + HD] = turned[j * rows_half : (j + 1) * rows_half]

    def to_core(c, i):
        return remote(
            proj16.at[c, 1 - core, i], r1.at[c, i], p1_ss.at[c, i], p1_rs.at[c, i],
            {"head": core_peer},
        )

    def to_row(c):
        return remote(s2.at[c], r2.at[c], p2_ss.at[c], p2_rs.at[c], {"head": row_peer})

    def forward(c):
        to_core(c, 0).wait_recv()
        s2[c] = (proj[c, core, 0] + r1[c, 0].astype(F32)).astype(BF16)
        to_row(c).start()

    def project(c, i):
        product = jnp.dot(att[i], w_v[c], preferred_element_type=F32)
        for side in range(2):
            part = product[side * piece : (side + 1) * piece]
            proj[c, side, i] = part
            proj16[c, side, i] = part.astype(BF16)
        to_core(c, i).start()

    finish(0)
    for c in range(PARTS):
        w_copy(c).wait()
        project(c, 0)
        if c > 0:
            forward(c - 1)
    forward(PARTS - 1)
    finish(1)
    for c in range(PARTS):
        project(c, 1)
    for c in range(PARTS):
        to_core(c, 1).wait_recv()
        to_row(c).wait_recv()
        out_ref[:, c * cols : (c + 1) * cols] = (
            proj[c, core, 1] + r1[c, 1].astype(F32) + r2[c].astype(F32)
        ).astype(BF16)

    for k in range(1, n):
        meta_send(k).wait_send()
    for copy in far_copies + back_copies:
        copy.wait_send()
    for copy in prev_copies:
        @pl.when(me < n - 1)
        def _(copy=copy):
            copy.wait_send()
    for x in range(GROUPS):
        def sent(k, _, x=x):
            kv_send(x, k).wait_send()
            return 0

        lax.fori_loop(1, half, sent, 0)
    for c in range(PARTS):
        to_core(c, 0).wait_send()
        to_core(c, 1).wait_send()
        to_row(c).wait_send()


def shards(
    queries, keys_new, values_new, cache_keys, cache_values, block_list, block_count, out_weight
):
    n = lax.axis_size("ctx")
    n_head = lax.axis_size("head")
    kvh = keys_new.shape[1] // HD
    group = queries.shape[1] // keys_new.shape[1]
    half = n // GROUPS
    width = group * BLOCK // 2
    d_in, d_out = out_weight.shape
    cols = d_out // PARTS
    piece = BLOCK // n_head
    vmem, any_space = pl.BlockSpec(memory_space=pltpu.VMEM), pl.BlockSpec(memory_space=pl.ANY)
    smem = pl.BlockSpec(memory_space=pltpu.SMEM)
    dma = pltpu.SemaphoreType.DMA
    keys_slot = CAP * BLOCK
    scratch = [
        pltpu.VMEM((n, 8, 128), jnp.int32),
        pltpu.VMEM((n, 8, 128), jnp.int32),
        pltpu.SMEM((n, 8, 128), jnp.int32),
        pltpu.VMEM((n, 8, 128), jnp.int32),
        pltpu.VMEM(queries.shape, BF16),
        pltpu.VMEM((2,) + keys_new.shape, BF16),
        pltpu.VMEM((GROUPS, kvh, 2, width, HD), BF16),
        pltpu.VMEM((GROUPS, half, kvh, 2, keys_slot, HD), BF16),
        pltpu.VMEM((GROUPS + 1, half, kvh, 2, keys_slot, HD), BF16),
        pltpu.VMEM((GROUPS, kvh, 2, HD, width), F32),
        pltpu.VMEM((GROUPS, 2, 8, width), F32),
        pltpu.VMEM((2, kvh, HD, width), BF16),
        pltpu.VMEM((2, kvh, HD, width), BF16),
        pltpu.VMEM((2, 8, width), F32),
        pltpu.VMEM((2, BLOCK // 2, d_in), BF16),
        pltpu.VMEM((PARTS, d_in, cols), BF16),
        pltpu.VMEM((PARTS, 2, n_head // 2, piece, cols), F32),
        pltpu.VMEM((PARTS, 2, n_head // 2, piece, cols), BF16),
        pltpu.VMEM((PARTS, n_head // 2, piece, cols), BF16),
        pltpu.VMEM((PARTS, piece, cols), BF16),
        pltpu.VMEM((PARTS, piece, cols), BF16),
        dma((n,)), dma((n,)), dma((n,)),
        dma((GROUPS, half)), dma((GROUPS + 1, half)),
        dma((2,)), dma((2,)), dma((2,)), dma((2,)), dma((2, 2)), dma((2, 2)),
        dma((PARTS,)), dma((PARTS, 2)), dma((PARTS, 2)), dma((PARTS,)), dma((PARTS,)),
    ]
    return pl.pallas_call(
        functools.partial(kernel, n, n_head, kvh, group),
        out_shape=jax.ShapeDtypeStruct((piece, d_out), BF16),
        in_specs=[vmem, smem] + [vmem] * 5 + [any_space],
        out_specs=vmem,
        scratch_shapes=scratch,
        compiler_params=pltpu.CompilerParams(
            collective_id=0, has_side_effects=True, vmem_limit_bytes=56 * 2**20
        ),
    )(
        block_list.reshape(kvh, -1), block_count.reshape(1, kvh),
        queries, keys_new, values_new,
        cache_keys.reshape(CB_DEV, BLOCK, -1), cache_values.reshape(CB_DEV, BLOCK, -1), out_weight,
    )


def solution(mesh):
    return jax.shard_map(
        shards,
        mesh=mesh,
        in_specs=(
            P("ctx", "head"),
            P("ctx", "head"),
            P("ctx", "head"),
            P("ctx", "head"),
            P("ctx", "head"),
            P("head", "ctx", None),
            P("head", "ctx"),
            P("head", None),
        ),
        out_specs=P(("ctx", "head"), None),
        check_vma=False,
    )
```

```python
import functools

import jax
import jax.numpy as jnp
from jax import lax
from jax.experimental import pallas as pl
from jax.experimental.pallas import tpu as pltpu
from jax.sharding import PartitionSpec as P

HD = 128
BLOCK = 128
CAP = 2
CB_DEV = 8
GROUPS = 2
PARTS = 4
NEG = -1e30
EXP2_SCALE = HD**-0.5 * 1.4426950408889634
F32 = jnp.float32
BF16 = jnp.bfloat16


def remote(src, dst, send_sem, recv_sem, device):
    return pltpu.make_async_remote_copy(
        src_ref=src,
        dst_ref=dst,
        send_sem=send_sem,
        recv_sem=recv_sem,
        device_id=device,
        device_id_type=pl.DeviceIdType.MESH,
    )


def kernel(
    n, n_head, kvh, group,
    list_ref, count_ref, q_ref, kn_ref, vn_ref, ck_ref, cv_ref, w_hbm,
    out_ref,
    table, meta, meta_s, far_table, far_q, prev, qstack, sendb, recvb, acc, stat,
    part_out, part_in, stat_in, att, w_v, proj, proj16, r1, s2, r2,
    meta_ss, meta_rs, smem_s, kv_ss, kv_rs, prev_ss, prev_rs, far_ss, far_rs,
    back_ss, back_rs, w_sem, p1_ss, p1_rs, p2_ss, p2_rs,
):
    me = lax.axis_index("ctx")
    hi = lax.axis_index("head")
    half = n // GROUPS
    mypos = lax.rem(me, half)
    base = me - mypos
    mirror = lax.rem(me + half, n)
    cols = w_v.shape[2]
    core = lax.rem(hi, 2)
    row = hi // 2
    core_peer = hi + 1 - 2 * core
    row_peer = lax.rem(hi + 2, n_head)
    sides = (1 - row, row)
    piece = BLOCK // n_head
    rows_half = BLOCK // 2

    def w_copy(c):
        return pltpu.make_async_copy(
            w_hbm.at[:, pl.ds(c * cols, cols)], w_v.at[c], w_sem.at[c]
        )

    barrier = pltpu.get_barrier_semaphore()
    for k in range(1, n):
        pl.semaphore_signal(
            barrier, inc=1, device_id={"ctx": lax.rem(me + k, n)},
            device_id_type=pl.DeviceIdType.MESH,
        )
    for k in range(1, n_head):
        pl.semaphore_signal(
            barrier, inc=1, device_id={"head": lax.rem(hi + k, n_head)},
            device_id_type=pl.DeviceIdType.MESH,
        )

    blk = list_ref[...]
    lane = lax.broadcasted_iota(jnp.int32, blk.shape, 1)
    head = lax.broadcasted_iota(jnp.int32, blk.shape, 0)
    used = jnp.full_like(blk, -1)
    for h in range(kvh):
        used = jnp.where((head == h) & (lane < count_ref[0, h]), blk, used)
    for o in range(n):
        mine = (used >= o * CB_DEV) & (used < (o + 1) * CB_DEV)
        first = jnp.min(jnp.where(mine, used - o * CB_DEV, CB_DEV - 1), axis=1, keepdims=True)
        last = jnp.max(jnp.where(mine, used - o * CB_DEV, 0), axis=1, keepdims=True)
        two = (last > first).astype(jnp.int32)
        table[o, 0:kvh, :] = jnp.broadcast_to(first, (kvh, 128))
        table[o, kvh : 2 * kvh, :] = jnp.broadcast_to(last, (kvh, 128))
        table[o, 2 * kvh : 3 * kvh, :] = jnp.broadcast_to(two, (kvh, 128))

    pl.semaphore_wait(barrier, n - 1 + n_head - 1)

    def meta_send(k):
        d = lax.rem(me + k, n)
        return remote(table.at[d], meta.at[me], meta_ss.at[k], meta_rs.at[me], {"ctx": d})

    def meta_recv(d):
        return remote(table.at[d], meta.at[d], meta_ss.at[0], meta_rs.at[d], {"ctx": mirror})

    for k in range(1, n):
        meta_send(k).start()
    far_copies = []
    if GROUPS == 2:
        far_copies = [
            remote(table, far_table, far_ss.at[0], far_rs.at[0], {"ctx": mirror}),
            remote(q_ref, far_q, far_ss.at[1], far_rs.at[1], {"ctx": mirror}),
        ]
    for copy in far_copies:
        copy.start()
    nxt = lax.rem(me + 1, n)
    prev_copies = [
        remote(kn_ref, prev.at[0], prev_ss.at[0], prev_rs.at[0], {"ctx": nxt}),
        remote(vn_ref, prev.at[1], prev_ss.at[1], prev_rs.at[1], {"ctx": nxt}),
    ]

    for copy in prev_copies:
        @pl.when(me < n - 1)
        def _(copy=copy):
            copy.start()

    def own_smem():
        return pltpu.make_async_copy(table.at[me], meta_s.at[me], smem_s.at[me])

    own_smem().start()

    def smem_copy(d):
        return pltpu.make_async_copy(meta.at[d], meta_s.at[d], smem_s.at[d])

    def partner(k):
        place, total = 1, 0
        while place < half:
            a, b = lax.rem(mypos // place, 2), lax.rem(k // place, 2)
            total = total + place * (a + b - 2 * a * b)
            place *= 2
        return total

    def target(x, k):
        pi = partner(lax.rem(half - k, half))
        p = base + pi
        d = p if x == 0 else lax.rem(p + half, n)
        return pi, p, d

    def gather(d, dst):
        for h in range(kvh):
            for s in range(CAP):
                index = meta_s[d, s * kvh + h, 0]
                cut = slice(h * HD, (h + 1) * HD)
                dst[h, 0, s * BLOCK : (s + 1) * BLOCK, :] = ck_ref[index, :, cut]
                dst[h, 1, s * BLOCK : (s + 1) * BLOCK, :] = cv_ref[index, :, cut]

    half_of = me // half
    top = mypos // (half // 2)
    inner = half_of * (1 - top) + (1 - half_of) * top

    def kv_send(x, k):
        pi, p, d = target(x, k)
        direct = x * inner * lax.div(half - k, half // 2)
        return remote(
            sendb.at[x, pi], recvb.at[x + direct, mypos],
            kv_ss.at[x, pi], kv_rs.at[x + direct, mypos], {"ctx": p + direct * (d - p)},
        )

    def kv_recv(x, k):
        pi, p, _ = target(0, k)
        return pi, remote(
            sendb.at[0, pi], recvb.at[x, pi], kv_ss.at[0, pi], kv_rs.at[x, pi], {"ctx": p}
        )

    order = list(range(GROUPS))[::-1]
    for x in order:
        def fetch(k, _, x=x):
            _, _, d = target(x, k)
            meta_recv(d).wait_recv()
            smem_copy(d).start()
            return 0

        lax.fori_loop(1, half, fetch, 0)
    if GROUPS == 2:
        meta_recv(mirror).wait_recv()
        smem_copy(mirror).start()
    for x in order:
        def give(k, _, x=x):
            pi, _, d = target(x, k)
            smem_copy(d).wait()
            gather(d, sendb.at[x, pi])
            kv_send(x, k).start()
            return 0

        lax.fori_loop(1, half, give, 0)

    for copy_c in range(PARTS):
        w_copy(copy_c).start()
    own_smem().wait()
    gather(me, recvb.at[0, mypos])
    if GROUPS == 2:
        smem_copy(mirror).wait()
        gather(mirror, recvb.at[1, mypos])

    width = group * rows_half

    def stack(x, ref):
        for h in range(kvh):
            for j in range(group):
                column = (h * group + j) * HD
                for f in range(2):
                    qstack[x, h, f, j * rows_half : (j + 1) * rows_half, :] = ref[
                        f * rows_half : (f + 1) * rows_half, column : column + HD
                    ]

    def attend(x, h, f, keys, values, mask):
        scores = lax.dot_general(
            keys, qstack[x, h, f], (((1,), (1,)), ((), ())), preferred_element_type=F32
        )
        scores = mask(scores)
        old_max = stat[x, f, h : h + 1, :]
        new_max = jnp.maximum(old_max, jnp.max(scores, axis=0, keepdims=True))
        weights = jnp.exp2((scores - new_max) * EXP2_SCALE)
        fade = jnp.exp2((old_max - new_max) * EXP2_SCALE)
        total = stat[x, f, kvh + h : kvh + h + 1, :] * fade
        stat[x, f, h : h + 1, :] = new_max
        stat[x, f, kvh + h : kvh + h + 1, :] = total + jnp.sum(weights, axis=0, keepdims=True)
        mixture = lax.dot_general(
            values, weights.astype(BF16), (((0,), (0,)), ((), ())), preferred_element_type=F32
        )
        acc[x, h, f] = acc[x, h, f] * fade + mixture

    def attend_cache(x, pi, halves=(0, 1)):
        flags = far_table if x == 1 else table
        owner = lax.rem(base + half, n) + pi if x == 2 else base + pi
        for f in halves:
            for h in range(kvh):
                two = flags[owner, 2 * kvh + h : 2 * kvh + h + 1, :]
                two = jnp.concatenate([two] * (width // 128), axis=1)

                def mask(scores, two=two):
                    return jnp.concatenate(
                        [scores[:BLOCK], jnp.where(two > 0, scores[BLOCK:], NEG)], axis=0
                    )

                attend(x % 2, h, f, recvb[x, pi, h, 0], recvb[x, pi, h, 1], mask)

    def attend_arrivals(x, first, stop):
        def step(k, _):
            pi, copy = kv_recv(x, k)
            copy.wait_recv()
            attend_cache(x, pi)
            return 0

        lax.fori_loop(first, stop, step, 0)

    stat[:, :, 0:kvh, :] = jnp.full((GROUPS, 2, kvh, width), NEG, F32)
    stat[:, :, kvh:, :] = jnp.zeros((GROUPS, 2, stat.shape[2] - kvh, width), F32)
    acc[...] = jnp.zeros_like(acc)
    stack(0, q_ref)

    def causal(f, scores):
        key = lax.broadcasted_iota(jnp.int32, scores.shape, 0)
        lane = lax.broadcasted_iota(jnp.int32, scores.shape, 1)
        return jnp.where(key <= f * rows_half + (lane & (rows_half - 1)), scores, NEG)

    for h in range(kvh):
        cut = slice(h * HD, (h + 1) * HD)
        for f in range(2):
            attend(0, h, f, kn_ref[:, cut], vn_ref[:, cut], functools.partial(causal, f))
    attend_cache(0, mypos)

    back_copies = []
    if GROUPS == 2:
        for copy in far_copies:
            copy.wait_recv()
        stack(1, far_q)
        attend_cache(1, mypos)

        @pl.when(inner == 1)
        def _():
            attend_arrivals(1, 1, half // 2 + 1)

        attend_arrivals(1, half // 2 + 1, half - 1)
        pi, copy = kv_recv(1, half - 1)
        copy.wait_recv()
        for i, f in enumerate(sides):
            attend_cache(1, pi, [f])
            for h in range(kvh):
                part_out[f, h] = acc[1, h, f].astype(BF16)
            pair = [
                remote(
                    stat.at[1, f], stat_in.at[f], back_ss.at[i, 0], back_rs.at[i, 0],
                    {"ctx": mirror},
                ),
                remote(
                    part_out.at[f], part_in.at[f], back_ss.at[i, 1], back_rs.at[i, 1],
                    {"ctx": mirror},
                ),
            ]
            for copy in pair:
                copy.start()
            back_copies += pair

    @pl.when(me > 0)
    def _():
        for copy in prev_copies:
            copy.wait_recv()
        for h in range(kvh):
            cut = slice(h * HD, (h + 1) * HD)
            for f in range(2):
                attend(0, h, f, prev[0, :, cut], prev[1, :, cut], lambda scores: scores)

    if GROUPS == 2:
        @pl.when(inner == 1)
        def _():
            attend_arrivals(2, 1, half // 2 + 1)

    attend_arrivals(0, 1, half)

    def finish(i):
        f = sides[i]
        for copy in back_copies[2 * i : 2 * i + 2]:
            copy.wait_recv()
        for h in range(kvh):
            own = acc[0, h, f]
            total = stat[0, f, kvh + h : kvh + h + 1, :]
            if GROUPS == 2:
                here, there = stat[0, f, h : h + 1, :], stat_in[f, h : h + 1, :]
                top = jnp.maximum(here, there)
                fade_here = jnp.exp2((here - top) * EXP2_SCALE)
                fade_there = jnp.exp2((there - top) * EXP2_SCALE)
                own = own * fade_here + part_in[f, h].astype(F32) * fade_there
                total = total * fade_here + stat_in[f, kvh + h : kvh + h + 1, :] * fade_there
            turned = (own / total).T.astype(BF16)
            for j in range(group):
                column = (h * group + j) * HD
                att[i, :, column : column + HD] = turned[j * rows_half : (j + 1) * rows_half]

    def to_core(c, i):
        return remote(
            proj16.at[c, 1 - core, i], r1.at[c, i], p1_ss.at[c, i], p1_rs.at[c, i],
            {"head": core_peer},
        )

    def to_row(c):
        return remote(s2.at[c], r2.at[c], p2_ss.at[c], p2_rs.at[c], {"head": row_peer})

    def forward(c):
        to_core(c, 0).wait_recv()
        s2[c] = (proj[c, core, 0] + r1[c, 0].astype(F32)).astype(BF16)
        to_row(c).start()

    def project(c, i):
        product = jnp.dot(att[i], w_v[c], preferred_element_type=F32)
        for side in range(2):
            part = product[side * piece : (side + 1) * piece]
            proj[c, side, i] = part
            proj16[c, side, i] = part.astype(BF16)
        to_core(c, i).start()

    finish(0)
    for c in range(PARTS):
        w_copy(c).wait()
        project(c, 0)
        if c > 0:
            forward(c - 1)
    forward(PARTS - 1)
    finish(1)
    for c in range(PARTS):
        project(c, 1)
    for c in range(PARTS):
        to_core(c, 1).wait_recv()
        to_row(c).wait_recv()
        out_ref[:, c * cols : (c + 1) * cols] = (
            proj[c, core, 1] + r1[c, 1].astype(F32) + r2[c].astype(F32)
        ).astype(BF16)

    for k in range(1, n):
        meta_send(k).wait_send()
    for copy in far_copies + back_copies:
        copy.wait_send()
    for copy in prev_copies:
        @pl.when(me < n - 1)
        def _(copy=copy):
            copy.wait_send()
    for x in range(GROUPS):
        def sent(k, _, x=x):
            kv_send(x, k).wait_send()
            return 0

        lax.fori_loop(1, half, sent, 0)
    for c in range(PARTS):
        to_core(c, 0).wait_send()
        to_core(c, 1).wait_send()
        to_row(c).wait_send()


def shards(
    queries, keys_new, values_new, cache_keys, cache_values, block_list, block_count, out_weight
):
    n = lax.axis_size("ctx")
    n_head = lax.axis_size("head")
    kvh = keys_new.shape[1] // HD
    group = queries.shape[1] // keys_new.shape[1]
    half = n // GROUPS
    width = group * BLOCK // 2
    d_in, d_out = out_weight.shape
    cols = d_out // PARTS
    piece = BLOCK // n_head
    vmem, any_space = pl.BlockSpec(memory_space=pltpu.VMEM), pl.BlockSpec(memory_space=pl.ANY)
    smem = pl.BlockSpec(memory_space=pltpu.SMEM)
    dma = pltpu.SemaphoreType.DMA
    keys_slot = CAP * BLOCK
    scratch = [
        pltpu.VMEM((n, 8, 128), jnp.int32),
        pltpu.VMEM((n, 8, 128), jnp.int32),
        pltpu.SMEM((n, 8, 128), jnp.int32),
        pltpu.VMEM((n, 8, 128), jnp.int32),
        pltpu.VMEM(queries.shape, BF16),
        pltpu.VMEM((2,) + keys_new.shape, BF16),
        pltpu.VMEM((GROUPS, kvh, 2, width, HD), BF16),
        pltpu.VMEM((GROUPS, half, kvh, 2, keys_slot, HD), BF16),
        pltpu.VMEM((GROUPS + 1, half, kvh, 2, keys_slot, HD), BF16),
        pltpu.VMEM((GROUPS, kvh, 2, HD, width), F32),
        pltpu.VMEM((GROUPS, 2, 8, width), F32),
        pltpu.VMEM((2, kvh, HD, width), BF16),
        pltpu.VMEM((2, kvh, HD, width), BF16),
        pltpu.VMEM((2, 8, width), F32),
        pltpu.VMEM((2, BLOCK // 2, d_in), BF16),
        pltpu.VMEM((PARTS, d_in, cols), BF16),
        pltpu.VMEM((PARTS, 2, n_head // 2, piece, cols), F32),
        pltpu.VMEM((PARTS, 2, n_head // 2, piece, cols), BF16),
        pltpu.VMEM((PARTS, n_head // 2, piece, cols), BF16),
        pltpu.VMEM((PARTS, piece, cols), BF16),
        pltpu.VMEM((PARTS, piece, cols), BF16),
        dma((n,)), dma((n,)), dma((n,)),
        dma((GROUPS, half)), dma((GROUPS + 1, half)),
        dma((2,)), dma((2,)), dma((2,)), dma((2,)), dma((2, 2)), dma((2, 2)),
        dma((PARTS,)), dma((PARTS, 2)), dma((PARTS, 2)), dma((PARTS,)), dma((PARTS,)),
    ]
    return pl.pallas_call(
        functools.partial(kernel, n, n_head, kvh, group),
        out_shape=jax.ShapeDtypeStruct((piece, d_out), BF16),
        in_specs=[vmem, smem] + [vmem] * 5 + [any_space],
        out_specs=vmem,
        scratch_shapes=scratch,
        compiler_params=pltpu.CompilerParams(
            collective_id=0, has_side_effects=True, vmem_limit_bytes=56 * 2**20
        ),
    )(
        block_list.reshape(kvh, -1), block_count.reshape(1, kvh),
        queries, keys_new, values_new,
        cache_keys.reshape(CB_DEV, BLOCK, -1), cache_values.reshape(CB_DEV, BLOCK, -1), out_weight,
    )


def solution(mesh):
    return jax.shard_map(
        shards,
        mesh=mesh,
        in_specs=(
            P("ctx", "head"),
            P("ctx", "head"),
            P("ctx", "head"),
            P("ctx", "head"),
            P("ctx", "head"),
            P("head", "ctx", None),
            P("head", "ctx"),
            P("head", None),
        ),
        out_specs=P(("ctx", "head"), None),
        check_vma=False,
    )
```

```python
import functools

import jax
import jax.numpy as jnp
from jax import lax
from jax.experimental import pallas as pl
from jax.experimental.pallas import tpu as pltpu
from jax.sharding import PartitionSpec as P

HD = 128
BLOCK = 128
CAP = 2
CB_DEV = 8
GROUPS = 2
PARTS = 4
NEG = -1e30
EXP2_SCALE = HD**-0.5 * 1.4426950408889634
F32 = jnp.float32
BF16 = jnp.bfloat16


def remote(src, dst, send_sem, recv_sem, device):
    return pltpu.make_async_remote_copy(
        src_ref=src,
        dst_ref=dst,
        send_sem=send_sem,
        recv_sem=recv_sem,
        device_id=device,
        device_id_type=pl.DeviceIdType.MESH,
    )


def kernel(
    n, n_head, kvh, group,
    list_ref, count_ref, q_ref, kn_ref, vn_ref, ck_ref, cv_ref, w_hbm,
    out_ref,
    table, meta, meta_s, far_table, far_q, prev, qstack, sendb, recvb, acc, stat,
    part_out, part_in, stat_in, att, w_v, proj, proj16, r1, s2, r2,
    meta_ss, meta_rs, smem_s, kv_ss, kv_rs, prev_ss, prev_rs, far_ss, far_rs,
    back_ss, back_rs, w_sem, p1_ss, p1_rs, p2_ss, p2_rs,
):
    me = lax.axis_index("ctx")
    hi = lax.axis_index("head")
    half = n // GROUPS
    mypos = lax.rem(me, half)
    base = me - mypos
    mirror = lax.rem(me + half, n)
    cols = w_v.shape[2]
    core = lax.rem(hi, 2)
    row = hi // 2
    core_peer = hi + 1 - 2 * core
    row_peer = lax.rem(hi + 2, n_head)
    sides = (1 - row, row)
    piece = BLOCK // n_head
    rows_half = BLOCK // 2

    def w_copy(c):
        return pltpu.make_async_copy(
            w_hbm.at[:, pl.ds(c * cols, cols)], w_v.at[c], w_sem.at[c]
        )

    barrier = pltpu.get_barrier_semaphore()
    for k in range(1, n):
        pl.semaphore_signal(
            barrier, inc=1, device_id={"ctx": lax.rem(me + k, n)},
            device_id_type=pl.DeviceIdType.MESH,
        )
    for k in range(1, n_head):
        pl.semaphore_signal(
            barrier, inc=1, device_id={"head": lax.rem(hi + k, n_head)},
            device_id_type=pl.DeviceIdType.MESH,
        )

    blk = list_ref[...]
    lane = lax.broadcasted_iota(jnp.int32, blk.shape, 1)
    head = lax.broadcasted_iota(jnp.int32, blk.shape, 0)
    used = jnp.full_like(blk, -1)
    for h in range(kvh):
        used = jnp.where((head == h) & (lane < count_ref[0, h]), blk, used)
    for o in range(n):
        mine = (used >= o * CB_DEV) & (used < (o + 1) * CB_DEV)
        first = jnp.min(jnp.where(mine, used - o * CB_DEV, CB_DEV - 1), axis=1, keepdims=True)
        last = jnp.max(jnp.where(mine, used - o * CB_DEV, 0), axis=1, keepdims=True)
        two = (last > first).astype(jnp.int32)
        table[o, 0:kvh, :] = jnp.broadcast_to(first, (kvh, 128))
        table[o, kvh : 2 * kvh, :] = jnp.broadcast_to(last, (kvh, 128))
        table[o, 2 * kvh : 3 * kvh, :] = jnp.broadcast_to(two, (kvh, 128))

    pl.semaphore_wait(barrier, n - 1 + n_head - 1)

    def meta_send(k):
        d = lax.rem(me + k, n)
        return remote(table.at[d], meta.at[me], meta_ss.at[k], meta_rs.at[me], {"ctx": d})

    def meta_recv(d):
        return remote(table.at[d], meta.at[d], meta_ss.at[0], meta_rs.at[d], {"ctx": mirror})

    for k in range(1, n):
        meta_send(k).start()
    far_copies = []
    if GROUPS == 2:
        far_copies = [
            remote(table, far_table, far_ss.at[0], far_rs.at[0], {"ctx": mirror}),
            remote(q_ref, far_q, far_ss.at[1], far_rs.at[1], {"ctx": mirror}),
        ]
    for copy in far_copies:
        copy.start()
    nxt = lax.rem(me + 1, n)
    prev_copies = [
        remote(kn_ref, prev.at[0], prev_ss.at[0], prev_rs.at[0], {"ctx": nxt}),
        remote(vn_ref, prev.at[1], prev_ss.at[1], prev_rs.at[1], {"ctx": nxt}),
    ]

    for copy in prev_copies:
        @pl.when(me < n - 1)
        def _(copy=copy):
            copy.start()

    def own_smem():
        return pltpu.make_async_copy(table.at[me], meta_s.at[me], smem_s.at[me])

    own_smem().start()

    def smem_copy(d):
        return pltpu.make_async_copy(meta.at[d], meta_s.at[d], smem_s.at[d])

    def partner(k):
        place, total = 1, 0
        while place < half:
            a, b = lax.rem(mypos // place, 2), lax.rem(k // place, 2)
            total = total + place * (a + b - 2 * a * b)
            place *= 2
        return total

    def target(x, k):
        pi = partner(lax.rem(half - k, half))
        p = base + pi
        d = p if x == 0 else lax.rem(p + half, n)
        return pi, p, d

    def gather(d, dst):
        for h in range(kvh):
            for s in range(CAP):
                index = meta_s[d, s * kvh + h, 0]
                cut = slice(h * HD, (h + 1) * HD)
                dst[h, 0, s * BLOCK : (s + 1) * BLOCK, :] = ck_ref[index, :, cut]
                dst[h, 1, s * BLOCK : (s + 1) * BLOCK, :] = cv_ref[index, :, cut]

    half_of = me // half
    top = mypos // (half // 2)
    inner = half_of * (1 - top) + (1 - half_of) * top

    def kv_send(x, k):
        pi, p, d = target(x, k)
        direct = x * inner * lax.div(half - k, half // 2)
        return remote(
            sendb.at[x, pi], recvb.at[x + direct, mypos],
            kv_ss.at[x, pi], kv_rs.at[x + direct, mypos], {"ctx": p + direct * (d - p)},
        )

    def kv_recv(x, k):
        pi, p, _ = target(0, k)
        return pi, remote(
            sendb.at[0, pi], recvb.at[x, pi], kv_ss.at[0, pi], kv_rs.at[x, pi], {"ctx": p}
        )

    order = list(range(GROUPS))[::-1]
    for x in order:
        def fetch(k, _, x=x):
            _, _, d = target(x, k)
            meta_recv(d).wait_recv()
            smem_copy(d).start()
            return 0

        lax.fori_loop(1, half, fetch, 0)
    if GROUPS == 2:
        meta_recv(mirror).wait_recv()
        smem_copy(mirror).start()
    for x in order:
        def give(step, _, x=x):
            k = half - step if x == 1 else step
            pi, _, d = target(x, k)
            smem_copy(d).wait()
            gather(d, sendb.at[x, pi])
            kv_send(x, k).start()
            return 0

        lax.fori_loop(1, half, give, 0)

    for copy_c in range(PARTS):
        w_copy(copy_c).start()
    own_smem().wait()
    gather(me, recvb.at[0, mypos])
    if GROUPS == 2:
        smem_copy(mirror).wait()
        gather(mirror, recvb.at[1, mypos])

    width = group * rows_half

    def stack(x, ref):
        for h in range(kvh):
            for j in range(group):
                column = (h * group + j) * HD
                for f in range(2):
                    qstack[x, h, f, j * rows_half : (j + 1) * rows_half, :] = ref[
                        f * rows_half : (f + 1) * rows_half, column : column + HD
                    ]

    def attend(x, h, f, keys, values, mask):
        scores = lax.dot_general(
            keys, qstack[x, h, f], (((1,), (1,)), ((), ())), preferred_element_type=F32
        )
        scores = mask(scores)
        old_max = stat[x, f, h : h + 1, :]
        new_max = jnp.maximum(old_max, jnp.max(scores, axis=0, keepdims=True))
        weights = jnp.exp2((scores - new_max) * EXP2_SCALE)
        fade = jnp.exp2((old_max - new_max) * EXP2_SCALE)
        total = stat[x, f, kvh + h : kvh + h + 1, :] * fade
        stat[x, f, h : h + 1, :] = new_max
        stat[x, f, kvh + h : kvh + h + 1, :] = total + jnp.sum(weights, axis=0, keepdims=True)
        mixture = lax.dot_general(
            values, weights.astype(BF16), (((0,), (0,)), ((), ())), preferred_element_type=F32
        )
        acc[x, h, f] = acc[x, h, f] * fade + mixture

    def attend_cache(x, pi, halves=(0, 1)):
        flags = far_table if x == 1 else table
        owner = lax.rem(base + half, n) + pi if x == 2 else base + pi
        for f in halves:
            for h in range(kvh):
                two = flags[owner, 2 * kvh + h : 2 * kvh + h + 1, :]
                two = jnp.concatenate([two] * (width // 128), axis=1)

                def mask(scores, two=two):
                    return jnp.concatenate(
                        [scores[:BLOCK], jnp.where(two > 0, scores[BLOCK:], NEG)], axis=0
                    )

                attend(x % 2, h, f, recvb[x, pi, h, 0], recvb[x, pi, h, 1], mask)

    def attend_arrivals(x, first, stop):
        def step(k, _):
            pi, copy = kv_recv(x, k)
            copy.wait_recv()
            attend_cache(x, pi)
            return 0

        lax.fori_loop(first, stop, step, 0)

    stat[:, :, 0:kvh, :] = jnp.full((GROUPS, 2, kvh, width), NEG, F32)
    stat[:, :, kvh:, :] = jnp.zeros((GROUPS, 2, stat.shape[2] - kvh, width), F32)
    acc[...] = jnp.zeros_like(acc)
    stack(0, q_ref)

    def causal(f, scores):
        key = lax.broadcasted_iota(jnp.int32, scores.shape, 0)
        lane = lax.broadcasted_iota(jnp.int32, scores.shape, 1)
        return jnp.where(key <= f * rows_half + (lane & (rows_half - 1)), scores, NEG)

    for h in range(kvh):
        cut = slice(h * HD, (h + 1) * HD)
        for f in range(2):
            attend(0, h, f, kn_ref[:, cut], vn_ref[:, cut], functools.partial(causal, f))
    attend_cache(0, mypos)

    back_copies = []
    if GROUPS == 2:
        for copy in far_copies:
            copy.wait_recv()
        stack(1, far_q)
        attend_cache(1, mypos)

        @pl.when(inner == 1)
        def _():
            attend_arrivals(1, 1, half // 2 + 1)

        attend_arrivals(1, half // 2 + 1, half - 1)
        pi, copy = kv_recv(1, half - 1)
        copy.wait_recv()
        for i, f in enumerate(sides):
            attend_cache(1, pi, [f])
            for h in range(kvh):
                part_out[f, h] = acc[1, h, f].astype(BF16)
            pair = [
                remote(
                    stat.at[1, f], stat_in.at[f], back_ss.at[i, 0], back_rs.at[i, 0],
                    {"ctx": mirror},
                ),
                remote(
                    part_out.at[f], part_in.at[f], back_ss.at[i, 1], back_rs.at[i, 1],
                    {"ctx": mirror},
                ),
            ]
            for copy in pair:
                copy.start()
            back_copies += pair

    @pl.when(me > 0)
    def _():
        for copy in prev_copies:
            copy.wait_recv()
        for h in range(kvh):
            cut = slice(h * HD, (h + 1) * HD)
            for f in range(2):
                attend(0, h, f, prev[0, :, cut], prev[1, :, cut], lambda scores: scores)

    if GROUPS == 2:
        @pl.when(inner == 1)
        def _():
            attend_arrivals(2, 1, half // 2 + 1)

    attend_arrivals(0, 1, half)

    def finish(i):
        f = sides[i]
        for copy in back_copies[2 * i : 2 * i + 2]:
            copy.wait_recv()
        for h in range(kvh):
            own = acc[0, h, f]
            total = stat[0, f, kvh + h : kvh + h + 1, :]
            if GROUPS == 2:
                here, there = stat[0, f, h : h + 1, :], stat_in[f, h : h + 1, :]
                top = jnp.maximum(here, there)
                fade_here = jnp.exp2((here - top) * EXP2_SCALE)
                fade_there = jnp.exp2((there - top) * EXP2_SCALE)
                own = own * fade_here + part_in[f, h].astype(F32) * fade_there
                total = total * fade_here + stat_in[f, kvh + h : kvh + h + 1, :] * fade_there
            turned = (own / total).T.astype(BF16)
            for j in range(group):
                column = (h * group + j) * HD
                att[i, :, column : column + HD] = turned[j * rows_half : (j + 1) * rows_half]

    def to_core(c, i):
        return remote(
            proj16.at[c, 1 - core, i], r1.at[c, i], p1_ss.at[c, i], p1_rs.at[c, i],
            {"head": core_peer},
        )

    def to_row(c):
        return remote(s2.at[c], r2.at[c], p2_ss.at[c], p2_rs.at[c], {"head": row_peer})

    def forward(c):
        to_core(c, 0).wait_recv()
        s2[c] = (proj[c, core, 0] + r1[c, 0].astype(F32)).astype(BF16)
        to_row(c).start()

    def project(c, i):
        product = jnp.dot(att[i], w_v[c], preferred_element_type=F32)
        for side in range(2):
            part = product[side * piece : (side + 1) * piece]
            proj[c, side, i] = part
            proj16[c, side, i] = part.astype(BF16)
        to_core(c, i).start()

    finish(0)
    for c in range(PARTS):
        w_copy(c).wait()
        project(c, 0)
        if c > 0:
            forward(c - 1)
    forward(PARTS - 1)
    finish(1)
    for c in range(PARTS):
        project(c, 1)
    for c in range(PARTS):
        to_core(c, 1).wait_recv()
        to_row(c).wait_recv()
        out_ref[:, c * cols : (c + 1) * cols] = (
            proj[c, core, 1] + r1[c, 1].astype(F32) + r2[c].astype(F32)
        ).astype(BF16)

    for k in range(1, n):
        meta_send(k).wait_send()
    for copy in far_copies + back_copies:
        copy.wait_send()
    for copy in prev_copies:
        @pl.when(me < n - 1)
        def _(copy=copy):
            copy.wait_send()
    for x in range(GROUPS):
        def sent(k, _, x=x):
            kv_send(x, k).wait_send()
            return 0

        lax.fori_loop(1, half, sent, 0)
    for c in range(PARTS):
        to_core(c, 0).wait_send()
        to_core(c, 1).wait_send()
        to_row(c).wait_send()


def shards(
    queries, keys_new, values_new, cache_keys, cache_values, block_list, block_count, out_weight
):
    n = lax.axis_size("ctx")
    n_head = lax.axis_size("head")
    kvh = keys_new.shape[1] // HD
    group = queries.shape[1] // keys_new.shape[1]
    half = n // GROUPS
    width = group * BLOCK // 2
    d_in, d_out = out_weight.shape
    cols = d_out // PARTS
    piece = BLOCK // n_head
    vmem, any_space = pl.BlockSpec(memory_space=pltpu.VMEM), pl.BlockSpec(memory_space=pl.ANY)
    smem = pl.BlockSpec(memory_space=pltpu.SMEM)
    dma = pltpu.SemaphoreType.DMA
    keys_slot = CAP * BLOCK
    scratch = [
        pltpu.VMEM((n, 8, 128), jnp.int32),
        pltpu.VMEM((n, 8, 128), jnp.int32),
        pltpu.SMEM((n, 8, 128), jnp.int32),
        pltpu.VMEM((n, 8, 128), jnp.int32),
        pltpu.VMEM(queries.shape, BF16),
        pltpu.VMEM((2,) + keys_new.shape, BF16),
        pltpu.VMEM((GROUPS, kvh, 2, width, HD), BF16),
        pltpu.VMEM((GROUPS, half, kvh, 2, keys_slot, HD), BF16),
        pltpu.VMEM((GROUPS + 1, half, kvh, 2, keys_slot, HD), BF16),
        pltpu.VMEM((GROUPS, kvh, 2, HD, width), F32),
        pltpu.VMEM((GROUPS, 2, 8, width), F32),
        pltpu.VMEM((2, kvh, HD, width), BF16),
        pltpu.VMEM((2, kvh, HD, width), BF16),
        pltpu.VMEM((2, 8, width), F32),
        pltpu.VMEM((2, BLOCK // 2, d_in), BF16),
        pltpu.VMEM((PARTS, d_in, cols), BF16),
        pltpu.VMEM((PARTS, 2, n_head // 2, piece, cols), F32),
        pltpu.VMEM((PARTS, 2, n_head // 2, piece, cols), BF16),
        pltpu.VMEM((PARTS, n_head // 2, piece, cols), BF16),
        pltpu.VMEM((PARTS, piece, cols), BF16),
        pltpu.VMEM((PARTS, piece, cols), BF16),
        dma((n,)), dma((n,)), dma((n,)),
        dma((GROUPS, half)), dma((GROUPS + 1, half)),
        dma((2,)), dma((2,)), dma((2,)), dma((2,)), dma((2, 2)), dma((2, 2)),
        dma((PARTS,)), dma((PARTS, 2)), dma((PARTS, 2)), dma((PARTS,)), dma((PARTS,)),
    ]
    return pl.pallas_call(
        functools.partial(kernel, n, n_head, kvh, group),
        out_shape=jax.ShapeDtypeStruct((piece, d_out), BF16),
        in_specs=[vmem, smem] + [vmem] * 5 + [any_space],
        out_specs=vmem,
        scratch_shapes=scratch,
        compiler_params=pltpu.CompilerParams(
            collective_id=0, has_side_effects=True, vmem_limit_bytes=56 * 2**20
        ),
    )(
        block_list.reshape(kvh, -1), block_count.reshape(1, kvh),
        queries, keys_new, values_new,
        cache_keys.reshape(CB_DEV, BLOCK, -1), cache_values.reshape(CB_DEV, BLOCK, -1), out_weight,
    )


def solution(mesh):
    return jax.shard_map(
        shards,
        mesh=mesh,
        in_specs=(
            P("ctx", "head"),
            P("ctx", "head"),
            P("ctx", "head"),
            P("ctx", "head"),
            P("ctx", "head"),
            P("head", "ctx", None),
            P("head", "ctx"),
            P("head", None),
        ),
        out_specs=P(("ctx", "head"), None),
        check_vma=False,
    )
```
